32 devices in a mesh: dp: 4 (over y, core), mem: 8 (over z, x).
Axes of the slice: x: 2, y: 2, z: 4, core: 2. Of those that a mesh axis runs over, the one named last changes fastest.
Arguments:
- slot_weight: bfloat16 [4096, 32], P(('dp', 'mem')), may hold values from -1.1953125 to 1.1953125
- slot_pos: int32 [4096, 32], P(('dp', 'mem')), may hold values from 0 to 255, as said below
- touched: int32 [32, 8, 32], P(('dp', 'mem')), may hold values from 0 to 255, as said below
- values: bfloat16 [2048, 4096], P('mem'), may hold values from -6 to 6
- cotangent: bfloat16 [4096, 4096], P(('dp', 'mem')), may hold values from -6 to 6
Outputs:
- memory_out: bfloat16 [4096, 4096], P(('dp', 'mem'))
- weight_grad: float32 [4096, 32], P(('dp', 'mem'))
- value_grad: float32 [2048, 4096], P('mem', 'dp')
The draws below stay inside these ranges and needn't reach their ends.
Inputs may be any that keep to these rules, and one draw needn't show every extreme that they name: `slot_pos`: each token's 32 positions are distinct. For each device and owner o, the positions used are o * 32 + j with j below a count c of 1 to 32; in each group of devices along mem, one owner has c = 32 from every device. `touched`: for each device and owner, the entries at the used positions are distinct; entries at unused positions are arbitrary rows.
All inputs are finite; a program needn't handle non-finite values.
Results may differ from the reference program's by a relative error of at most 0.001.
Values may be sent and summed in bfloat16 or wider, within the bound.
A program may use at most 256 MiB of HBM per device.

```python
import jax
import jax.numpy as jnp
from jax import lax

D = 4096
TOPK = 32
CAP = 32
TOK_DEV = 128
ROWS_DEV = 256
TOKENS = 4096
ROWS = 2048
N_DP = 4
N_MEM = 8


def live_counts(key):
    key = jax.random.fold_in(key, 101)
    key_hot, key_raw, key_full = jax.random.split(key, 3)
    hotness = jax.random.randint(key_hot, (N_DP, 1, N_MEM), 1, 5)
    raw = jax.random.randint(key_raw, (N_DP, N_MEM, N_MEM), 0, CAP)
    least = (TOPK + N_MEM - 1) // N_MEM
    counted = jnp.maximum(1 + raw * hotness // 2, least)
    counted = jnp.minimum(counted, CAP)
    fullest = jax.random.randint(key_full, (N_DP, 1, 1), 0, N_MEM)
    owners = jnp.arange(N_MEM, dtype=jnp.int32)[None, None, :]
    counted = jnp.where(owners == fullest, CAP, counted)
    return counted.reshape(N_DP * N_MEM, N_MEM)


def draw_touched(key, part):
    key = jax.random.fold_in(key, 7)
    spread = 2 ** 30 // ROWS_DEV
    scores = jax.random.randint(key, (N_DP * N_MEM, N_MEM, ROWS_DEV), 0, spread) * ROWS_DEV
    scores = scores + jnp.arange(ROWS_DEV, dtype=jnp.int32)
    _, picked = lax.top_k(scores, CAP)
    return picked.astype(jnp.int32)


def draw_slot_pos(key, part):
    counted = live_counts(key)
    key = jax.random.fold_in(key, 11)
    places = N_MEM * CAP
    within = jnp.arange(CAP, dtype=jnp.int32)[None, None, :]
    valid = (within < counted[:, :, None]).reshape(N_DP * N_MEM, 1, places)
    spread = 2 ** 30 // places
    index = jnp.arange(places, dtype=jnp.int32)
    scores = jax.random.randint(key, (N_DP * N_MEM, TOK_DEV, places), 0, spread) * places + index
    scores = jnp.where(valid, scores, -1 - index)
    _, chosen = lax.top_k(scores, TOPK)
    return chosen.reshape(N_DP * N_MEM * TOK_DEV, TOPK).astype(jnp.int32)


def block_scale(stream_key, shape, pieces, low, high):
    gain, own = 1.0, jax.random.fold_in(stream_key, 6)
    for dim, shards_of in pieces:
        draws = jnp.exp(jax.random.uniform(jax.random.fold_in(own, dim), (shards_of,), jnp.float32, low / len(pieces), high / len(pieces)))
        gain = gain * jnp.repeat(draws, shape[dim] // shards_of).reshape([-1 if axis == dim else 1 for axis in range(len(shape))])
    return gain


def normal_values(own_key, dims, width, most, shards=(), kind=jnp.bfloat16):
    factor_of = block_scale(own_key, dims, shards, -0.22, 0.18) if shards else 1.0
    entries = jax.random.normal(own_key, dims, jnp.float32) * width * factor_of
    return jnp.minimum(jnp.maximum(entries, -most), most).astype(kind)


def setup_inputs(seed: int = 0) -> dict:
    keys = jax.random.split(jax.random.key(seed), 6)
    return {
        "slot_weight": normal_values(keys[0], (TOKENS, TOPK), 0.2, 1.1953125, ((0, 32),)),
        "slot_pos": draw_slot_pos(jax.random.fold_in(keys[5], 71), 0),
        "touched": draw_touched(jax.random.fold_in(keys[5], 71), 0),
        "values": normal_values(keys[3], (ROWS, D), 1.0, 6.0, ((0, 8),)),
        "cotangent": normal_values(keys[4], (TOKENS, D), 1.0, 6.0, ((0, 32),)),
    }


def reference(slot_weight, slot_pos, touched, values, cotangent):
    blocks = TOKENS // TOK_DEV
    pos_b = slot_pos.reshape(blocks, TOK_DEV, TOPK)
    wgt_b = slot_weight.reshape(blocks, TOK_DEV, TOPK)
    cot_b = cotangent.reshape(blocks, TOK_DEV, D)

    def one_block(table, inputs):
        pos, wgt, cot, lists = inputs
        owner = (pos // CAP).astype(jnp.int32)
        within = (pos % CAP).astype(jnp.int32)
        rows = owner * ROWS_DEV + lists[owner, within]
        picked = values[rows].astype(jnp.float32)
        weights = wgt.astype(jnp.float32)
        grads = cot.astype(jnp.float32)
        bag = jnp.einsum("tk,tkd->td", weights, picked)
        wgrad = jnp.einsum("td,tkd->tk", grads, picked)
        terms = weights[:, :, None] * grads[:, None, :]
        table = table.at[rows.reshape(-1)].add(terms.reshape(-1, D))
        return table, (bag.astype(jnp.bfloat16), wgrad)

    start = jnp.zeros((ROWS, D), jnp.float32)
    table, (bags, wgrads) = lax.scan(one_block, start, (pos_b, wgt_b, cot_b, touched))
    return bags.reshape(TOKENS, D), wgrads.reshape(TOKENS, TOPK), table
```

```python
import functools

import jax
import jax.numpy as jnp
from jax import lax
from jax.experimental import pallas as pl
from jax.experimental.pallas import tpu as pltpu
from jax.sharding import PartitionSpec as P

MESH = pl.DeviceIdType.MESH
STEPS = 32000.0


def iota(shape, axis):
    return lax.broadcasted_iota(jnp.int32, shape, axis)


def coded(x):
    top = jnp.max(jnp.abs(x), axis=1, keepdims=True)
    step = jnp.maximum(top * (1.0 / STEPS), 1e-30).astype(jnp.bfloat16).astype(jnp.float32)
    return jnp.round(x * (1.0 / step)).astype(jnp.int32).astype(jnp.int16), step


def pieces(q):
    full = q.astype(jnp.int32).astype(jnp.float32)
    high = full.astype(jnp.bfloat16)
    return high, (full - high.astype(jnp.float32)).astype(jnp.bfloat16)


def decoded_sum(hot, q):
    high, low = pieces(q)
    return jnp.dot(hot, high, preferred_element_type=jnp.float32) + jnp.dot(
        hot, low, preferred_element_type=jnp.float32
    )


def kernel(
    n_dp, n_mem,
    lists_ref, pos_ref, w_ref, cot_ref, values_ref,
    out_ref, wgrad_ref, vgrad_ref,
    dense_w, step_mine, step_got, lists_got, coded_mine, coded_got, hot, vals, picked, arrived,
    sum_mine, sum_coded, sum_got, sum_step, sum_step_got,
    list_ss, list_rs, step_ss, step_rs, grad_ss, grad_rs, val_ss, val_rs, pair_ss, pair_rs, own_sem,
):
    half = n_mem // 2
    group = n_dp * half
    cap = lists_ref.shape[1]
    toks, topk = pos_ref.shape
    rows = values_ref.shape[0]
    cols = cot_ref.shape[1] // n_dp
    spread = n_mem * cap
    bits = cap.bit_length() - 1
    dp = lax.axis_index("dp")
    mem = lax.axis_index("mem")
    here = lax.rem(mem, half)
    base = mem - here
    mirror = lax.rem(mem + half, n_mem)
    other_base = half - base
    me = dp * half + here

    def place(t):
        d = lax.rem(dp + 1 + t // half, n_dp)
        h = lax.rem(here + 1 + lax.rem(t, half), half)
        return d, h, d * half + h

    def every(fn, first=0, last=group - 1):
        def body(t, c):
            fn(*place(t))
            return c
        lax.fori_loop(first, last, body, 0)

    def remote(src, dst, ss, rs, d, m):
        return pltpu.make_async_remote_copy(
            src_ref=src, dst_ref=dst, send_sem=ss, recv_sem=rs, device_id=(d, m), device_id_type=MESH
        )

    barrier = pltpu.get_barrier_semaphore()
    every(lambda d, h, g: pl.semaphore_signal(barrier, inc=1, device_id=(d, base + h), device_id_type=MESH))
    pl.semaphore_signal(barrier, inc=1, device_id=(dp, mirror), device_id_type=MESH)

    my_cols = pl.ds(pl.multiple_of(dp * cols, cols), cols)
    own = pltpu.make_async_copy(values_ref.at[:, my_cols], vals.at[0], own_sem)
    own.start()
    lists_got[me] = lists_ref[...]

    lane = iota((toks, spread), 1)
    acc = jnp.zeros((toks, spread), jnp.float32)
    for k in range(topk):
        acc = jnp.where(pos_ref[:, k : k + 1] == lane, w_ref[:, k : k + 1].astype(jnp.float32), acc)
    dense_w[...] = acc.astype(jnp.bfloat16)

    pl.semaphore_wait(barrier, group)

    def list_copy(d, h, g):
        return remote(lists_ref, lists_got.at[me], list_ss.at[g], list_rs.at[me], d, base + h)

    every(lambda d, h, g: list_copy(d, h, g).start())
    pair_vals = remote(values_ref.at[:, my_cols], vals.at[1], pair_ss.at[0], pair_rs.at[0], dp, mirror)
    pair_vals.start()

    def grad_copy(o, d, h, g):
        m = (other_base if o else base) + h
        return remote(
            coded_mine.at[d, m], coded_got.at[o, me], grad_ss.at[o, g], grad_rs.at[o, me], d, base + h
        )

    def step_copy(d, h, g):
        return remote(step_mine.at[d], step_got.at[me], step_ss.at[g], step_rs.at[me], d, base + h)

    to_owner = (iota((n_mem, spread), 1) >> bits == iota((n_mem, spread), 0)).astype(jnp.bfloat16)
    to_lane = iota((spread, cap), 0) & (cap - 1) == iota((spread, cap), 1)
    for i in range(n_dp):
        d_now = lax.rem(dp + 1 + i, n_dp)
        block = cot_ref[:, pl.ds(pl.multiple_of(d_now * cols, cols), cols)]
        terms = lax.dot_general(
            dense_w[...], block, (((0,), (0,)), ((), ())), preferred_element_type=jnp.float32
        )
        q, step = coded(terms)
        coded_mine[d_now] = q.reshape(n_mem, cap, cols)
        step_mine[d_now] = jnp.dot(
            to_owner, jnp.where(to_lane, step, 0.0).astype(jnp.bfloat16), preferred_element_type=jnp.float32
        )
        first, last = i * half, min((i + 1) * half, group - 1)
        every(lambda d, h, g: step_copy(d, h, g).start(), first, last)
        every(lambda d, h, g: grad_copy(1, d, h, g).start(), first, last)
        every(lambda d, h, g: grad_copy(0, d, h, g).start(), first, last)
    step_got[me] = step_mine[dp]
    coded_got[0, me] = coded_mine[dp, mem]
    coded_got[1, me] = coded_mine[dp, mirror]

    every(lambda d, h, g: remote(lists_ref, lists_got.at[g], list_ss.at[g], list_rs.at[g], d, base + h).wait_recv())
    slots = group * cap
    fan = (iota((cap, slots), 1) & (cap - 1) == iota((cap, slots), 0)).astype(jnp.bfloat16)
    diag = iota((group, slots), 1) >> bits == iota((group, slots), 0)

    def along_lanes(table, m):
        pick = iota(table.shape, 1) == m
        part = jnp.sum(jnp.where(pick, table, 0.0), axis=1).astype(jnp.bfloat16)
        wide = jnp.dot(part, fan, preferred_element_type=jnp.float32)
        return jnp.sum(jnp.where(diag, wide, 0.0), axis=0, keepdims=True)

    lists_f = lists_got[...].astype(jnp.float32)
    row_of = iota((rows, slots), 0).astype(jnp.float32)

    def val_copy(o, d, h, g):
        m = mirror if o else mem
        return remote(
            picked.at[o, g], arrived.at[m, :, my_cols], val_ss.at[o, g], val_rs.at[o, me], d, base + h
        )

    some = min(group, 16)

    def select(o):
        def body(b, c):
            lanes = pl.ds(pl.multiple_of(b * some * cap, some * cap), some * cap)
            got = lax.dot_general(
                hot[o, :, lanes], vals[o], (((0,), (0,)), ((), ())), preferred_element_type=jnp.float32
            )
            picked[o, pl.ds(b * some, some)] = got.astype(jnp.bfloat16).reshape(some, cap, cols)
            return c
        lax.fori_loop(0, group // some, body, 0)

    for o, m in ((0, mem), (1, mirror)):
        hot[o] = (row_of == along_lanes(lists_f, m)).astype(jnp.bfloat16)
    own.wait()
    select(0)
    every(lambda d, h, g: val_copy(0, d, h, g).start())
    arrived[mem, :, my_cols] = picked[0, me]
    pair_vals.wait_recv()
    select(1)
    every(lambda d, h, g: val_copy(1, d, h, g).start())
    arrived[mirror, :, my_cols] = picked[1, me]

    every(lambda d, h, g: remote(step_mine.at[0], step_got.at[g], step_ss.at[g], step_rs.at[g], d, base + h).wait_recv())
    steps = step_got[...]

    def gathered(o, m):
        every(
            lambda d, h, g: remote(
                coded_mine.at[0, 0], coded_got.at[o, g], grad_ss.at[o, g], grad_rs.at[o, g], d, base + h
            ).wait_recv()
        )
        scaled = (hot[o].astype(jnp.float32) * along_lanes(steps, m)).astype(jnp.bfloat16)
        return decoded_sum(scaled, coded_got[o].reshape(slots, cols))

    q, step = coded(gathered(1, mirror))
    sum_coded[...] = q
    eye = iota((rows, rows), 0) == iota((rows, rows), 1)
    sum_step[...] = jnp.broadcast_to(jnp.sum(jnp.where(eye, step, 0.0), axis=0, keepdims=True), sum_step.shape)
    pair_step = remote(sum_step, sum_step_got, pair_ss.at[1], pair_rs.at[1], dp, mirror)
    pair_step.start()
    pair_sum = remote(sum_coded, sum_got, pair_ss.at[2], pair_rs.at[2], dp, mirror)
    pair_sum.start()
    sum_mine[...] = gathered(0, mem)

    def val_wait(o, d, h, g):
        m = (other_base if o else base) + h
        cols_d = pl.ds(pl.multiple_of(d * cols, cols), cols)
        remote(
            picked.at[o, g], arrived.at[m, :, cols_d], val_ss.at[o, g], val_rs.at[o, g], d, base + h
        ).wait_recv()

    every(lambda d, h, g: val_wait(0, d, h, g))
    every(lambda d, h, g: val_wait(1, d, h, g))

    def tokens(b, scores):
        at = pl.ds(pl.multiple_of(b * cols, cols), cols)
        table = arrived[:, :, at].reshape(spread, cols)
        out_ref[:, at] = jnp.dot(dense_w[...], table, preferred_element_type=jnp.float32).astype(out_ref.dtype)
        return scores + lax.dot_general(
            cot_ref[:, at], table, (((1,), (1,)), ((), ())), preferred_element_type=jnp.float32
        )

    scores = lax.fori_loop(0, n_dp, tokens, jnp.zeros((toks, spread), jnp.float32))
    slot = iota((toks, topk), 1)
    wgrad = jnp.zeros((toks, topk), jnp.float32)
    for k in range(topk):
        one = jnp.sum(jnp.where(pos_ref[:, k : k + 1] == lane, scores, 0.0), axis=1, keepdims=True)
        wgrad = jnp.where(slot == k, one, wgrad)
    wgrad_ref[...] = wgrad

    pair_step.wait_recv()
    pair_sum.wait_recv()
    scaled = jnp.where(eye, sum_step_got[0:1, :], 0.0).astype(jnp.bfloat16)
    vgrad_ref[...] = sum_mine[...] + decoded_sum(scaled, sum_got[...])

    every(lambda d, h, g: list_copy(d, h, g).wait_send())
    every(lambda d, h, g: step_copy(d, h, g).wait_send())
    for o in range(2):
        every(lambda d, h, g: grad_copy(o, d, h, g).wait_send())
        every(lambda d, h, g: val_copy(o, d, h, g).wait_send())
    pair_vals.wait_send()
    pair_step.wait_send()
    pair_sum.wait_send()


def on_device(n_dp, n_mem, slot_weight, slot_pos, touched, values, cotangent):
    toks, topk = slot_pos.shape
    lists = touched[0]
    cap = lists.shape[1]
    rows, width = values.shape
    cols = width // n_dp
    group = n_dp * n_mem // 2
    f32, bf16, i16 = jnp.float32, jnp.bfloat16, jnp.int16
    dma = pltpu.SemaphoreType.DMA
    vmem = pl.BlockSpec(memory_space=pltpu.VMEM)
    return pl.pallas_call(
        functools.partial(kernel, n_dp, n_mem),
        out_shape=(
            jax.ShapeDtypeStruct((toks, width), bf16),
            jax.ShapeDtypeStruct((toks, topk), f32),
            jax.ShapeDtypeStruct((rows, cols), f32),
        ),
        in_specs=[vmem, vmem, vmem, vmem, pl.BlockSpec(memory_space=pl.ANY)],
        out_specs=(vmem, vmem, vmem),
        scratch_shapes=[
            pltpu.VMEM((toks, n_mem * cap), bf16),
            pltpu.VMEM((n_dp, n_mem, cap), f32),
            pltpu.VMEM((group, n_mem, cap), f32),
            pltpu.VMEM((group, n_mem, cap), jnp.int32),
            pltpu.VMEM((n_dp, n_mem, cap, cols), i16),
            pltpu.VMEM((2, group, cap, cols), i16),
            pltpu.VMEM((2, rows, group * cap), bf16),
            pltpu.VMEM((2, rows, cols), bf16),
            pltpu.VMEM((2, group, cap, cols), bf16),
            pltpu.VMEM((n_mem, cap, width), bf16),
            pltpu.VMEM((rows, cols), f32),
            pltpu.VMEM((rows, cols), i16),
            pltpu.VMEM((rows, cols), i16),
            pltpu.VMEM((8, rows), f32),
            pltpu.VMEM((8, rows), f32),
            dma((group,)), dma((group,)),
            dma((group,)), dma((group,)),
            dma((2, group)), dma((2, group)),
            dma((2, group)), dma((2, group)),
            dma((3,)), dma((3,)),
            dma,
        ],
        compiler_params=pltpu.CompilerParams(
            collective_id=0, has_side_effects=True, vmem_limit_bytes=60 * 2**20
        ),
    )(lists, slot_pos, slot_weight, cotangent, values)


def solution(mesh):
    return jax.shard_map(
        functools.partial(on_device, mesh.shape["dp"], mesh.shape["mem"]),
        mesh=mesh,
        in_specs=(
            P(("dp", "mem"), None),
            P(("dp", "mem"), None),
            P(("dp", "mem"), None, None),
            P("mem", None),
            P(("dp", "mem"), None),
        ),
        out_specs=(P(("dp", "mem"), None), P(("dp", "mem"), None), P("mem", "dp")),
        check_vma=False,
    )
```

```python
import functools

import jax
import jax.numpy as jnp
from jax import lax
from jax.experimental import pallas as pl
from jax.experimental.pallas import tpu as pltpu
from jax.sharding import PartitionSpec as P

MESH = pl.DeviceIdType.MESH
STEPS = 32000.0


def iota(shape, axis):
    return lax.broadcasted_iota(jnp.int32, shape, axis)


def coded(x):
    top = jnp.max(jnp.abs(x), axis=1, keepdims=True)
    step = jnp.maximum(top * (1.0 / STEPS), 1e-30).astype(jnp.bfloat16).astype(jnp.float32)
    return jnp.round(x * (1.0 / step)).astype(jnp.int32).astype(jnp.int16), step


def pieces(q):
    full = q.astype(jnp.int32).astype(jnp.float32)
    high = full.astype(jnp.bfloat16)
    return high, (full - high.astype(jnp.float32)).astype(jnp.bfloat16)


def decoded_sum(hot, q):
    high, low = pieces(q)
    return jnp.dot(hot, high, preferred_element_type=jnp.float32) + jnp.dot(
        hot, low, preferred_element_type=jnp.float32
    )


def kernel(
    n_dp, n_mem, n_x,
    lists_ref, pos_ref, w_ref, cot_ref, values_ref,
    out_ref, wgrad_ref, vgrad_ref,
    dense_w, step_mine, step_got, lists_got, coded_mine, coded_got, hot, vals, picked, arrived,
    sum_mine, sum_coded, sum_got, sum_step, sum_step_got,
    list_ss, list_rs, step_ss, step_rs, grad_ss, grad_rs, val_ss, val_rs,
    line_ss, line_rs, sum_ss, sum_rs, own_sem,
):
    n_z = n_mem // n_x
    group = n_dp * n_x
    cap = lists_ref.shape[1]
    topk, toks = pos_ref.shape
    rows = values_ref.shape[0]
    cols = cot_ref.shape[1] // n_dp
    spread = n_mem * cap
    bits = cap.bit_length() - 1
    dp = lax.axis_index("dp")
    mem = lax.axis_index("mem")
    z = mem // n_x
    x = lax.rem(mem, n_x)
    me = dp * n_x + x
    has_below, has_above = z > 0, z < n_z - 1

    def place(t):
        d = lax.rem(dp + 1 + t // n_x, n_dp)
        h = lax.rem(x + 1 + lax.rem(t, n_x), n_x)
        return d, h, d * n_x + h

    def every(fn):
        def body(t, c):
            fn(*place(t))
            return c
        lax.fori_loop(0, group - 1, body, 0)

    def remote(src, dst, ss, rs, d, m):
        return pltpu.make_async_remote_copy(
            src_ref=src, dst_ref=dst, send_sem=ss, recv_sem=rs, device_id=(d, m), device_id_type=MESH
        )

    def plane(src, dst, ss, rs, d, h):
        return remote(src, dst, ss, rs, d, z * n_x + h)

    barrier = pltpu.get_barrier_semaphore()

    def greet(m):
        pl.semaphore_signal(barrier, inc=1, device_id=(dp, m), device_id_type=MESH)

    every(
        lambda d, h, g: pl.semaphore_signal(
            barrier, inc=1, device_id=(d, z * n_x + h), device_id_type=MESH
        )
    )
    pl.when(has_below)(lambda: greet(mem - n_x))
    pl.when(has_above)(lambda: greet(mem + n_x))

    my_cols = pl.ds(pl.multiple_of(dp * cols, cols), cols)
    own = pltpu.make_async_copy(values_ref.at[:, my_cols], vals.at[z], own_sem)
    own.start()
    lists_got[me] = lists_ref[...]

    place_of = iota((spread, toks), 0)
    acc = jnp.zeros((spread, toks), jnp.float32)
    weights = w_ref[...].astype(jnp.float32)
    for k in range(topk):
        acc = jnp.where(pos_ref[k : k + 1, :] == place_of, weights[k : k + 1, :], acc)
    dense_w[...] = acc.astype(jnp.bfloat16)

    pl.semaphore_wait(barrier, group - 1 + has_below.astype(jnp.int32) + has_above.astype(jnp.int32))

    def line_copy(k, up):
        way = 1 if up else 0
        return remote(
            vals.at[k], vals.at[k], line_ss.at[way, k], line_rs.at[k], dp, mem + n_x if up else mem - n_x
        )

    def pass_on(k, up):
        pl.when(has_above if up else has_below)(lambda: line_copy(k, up).start())

    def list_copy(d, h, g):
        return plane(lists_ref, lists_got.at[me], list_ss.at[g], list_rs.at[me], d, h)

    every(lambda d, h, g: list_copy(d, h, g).start())
    own.wait()
    pass_on(z, True)
    pass_on(z, False)

    def grad_copy(k, d, h, g):
        return plane(
            coded_mine.at[d, k * n_x + h], coded_got.at[k, me], grad_ss.at[k, g], grad_rs.at[k, me], d, h
        )

    def step_copy(d, h, g):
        return plane(step_mine.at[d], step_got.at[me], step_ss.at[g], step_rs.at[me], d, h)

    to_owner = (iota((n_mem, spread), 1) >> bits == iota((n_mem, spread), 0)).astype(jnp.bfloat16)
    to_lane = iota((spread, cap), 0) & (cap - 1) == iota((spread, cap), 1)

    def terms_of(d, c):
        block = cot_ref[:, pl.ds(pl.multiple_of(d * cols, cols), cols)]
        q, step = coded(jnp.dot(dense_w[...], block, preferred_element_type=jnp.float32))
        coded_mine[d] = q.reshape(n_mem, cap, cols)
        step_mine[d] = jnp.dot(
            to_owner, jnp.where(to_lane, step, 0.0).astype(jnp.bfloat16), preferred_element_type=jnp.float32
        )
        return c

    lax.fori_loop(0, n_dp, terms_of, 0)
    every(lambda d, h, g: step_copy(d, h, g).start())
    outer_first = [k for pair in zip(range(n_z), reversed(range(n_z))) for k in pair][:n_z]
    for k in outer_first:
        every(lambda d, h, g: grad_copy(k, d, h, g).start())
        coded_got[k, me] = coded_mine[dp, k * n_x + x]
    step_got[me] = step_mine[dp]

    every(lambda d, h, g: plane(lists_ref, lists_got.at[g], list_ss.at[g], list_rs.at[g], d, h).wait_recv())
    slots = group * cap
    fan = (iota((cap, slots), 1) & (cap - 1) == iota((cap, slots), 0)).astype(jnp.bfloat16)
    diag = iota((group, slots), 1) >> bits == iota((group, slots), 0)

    def along_lanes(table, m):
        pick = iota(table.shape, 1) == m
        part = jnp.sum(jnp.where(pick, table, 0.0), axis=1).astype(jnp.bfloat16)
        wide = jnp.dot(part, fan, preferred_element_type=jnp.float32)
        return jnp.sum(jnp.where(diag, wide, 0.0), axis=0, keepdims=True)

    row_of = iota((rows, slots), 0).astype(jnp.float32)

    def hot_of(k, c):
        lists_f = lists_got[...].astype(jnp.float32)
        hot[k] = (row_of == along_lanes(lists_f, k * n_x + x)).astype(jnp.bfloat16)
        return c

    lax.fori_loop(0, n_z, hot_of, 0)

    def val_copy(k, d, h, g):
        return plane(
            picked.at[k, g], arrived.at[k * n_x + x, :, my_cols], val_ss.at[k, g], val_rs.at[k, me], d, h
        )

    def select(k):
        got = lax.dot_general(
            hot[k], vals[k], (((0,), (0,)), ((), ())), preferred_element_type=jnp.float32
        )
        picked[k] = got.astype(jnp.bfloat16).reshape(group, cap, cols)
        every(lambda d, h, g: val_copy(k, d, h, g).start())
        arrived[k * n_x + x, :, my_cols] = picked[k, me]

    select(z)

    every(
        lambda d, h, g: plane(step_mine.at[0], step_got.at[g], step_ss.at[g], step_rs.at[g], d, h).wait_recv()
    )
    eye = iota((rows, rows), 0) == iota((rows, rows), 1)

    def gathered(k):
        every(
            lambda d, h, g: plane(
                coded_mine.at[0, 0], coded_got.at[k, g], grad_ss.at[k, g], grad_rs.at[k, g], d, h
            ).wait_recv()
        )
        scaled = (hot[k].astype(jnp.float32) * along_lanes(step_got[...], k * n_x + x)).astype(jnp.bfloat16)
        return decoded_sum(scaled, coded_got[k].reshape(slots, cols))

    def sum_copies(k, up):
        to = mem + n_x if up else mem - n_x
        at = jnp.where(k == z + 1, n_z, k) if up else k
        return (
            remote(sum_step.at[k], sum_step_got.at[at], sum_ss.at[0, k], sum_rs.at[0, at], dp, to),
            remote(sum_coded.at[k], sum_got.at[at], sum_ss.at[1, k], sum_rs.at[1, at], dp, to),
        )

    def received(at):
        remote(sum_step.at[0], sum_step_got.at[at], sum_ss.at[0, 0], sum_rs.at[0, at], dp, mem).wait_recv()
        remote(sum_coded.at[0], sum_got.at[at], sum_ss.at[1, 0], sum_rs.at[1, at], dp, mem).wait_recv()
        scaled = jnp.where(eye, sum_step_got[at][0:1, :], 0.0).astype(jnp.bfloat16)
        return decoded_sum(scaled, sum_got[at])

    def relay(k, up, first):
        sum_mine[...] = gathered(k)

        @pl.when(jnp.logical_not(first))
        def _():
            sum_mine[...] += received(k)

        q, step = coded(sum_mine[...])
        sum_coded[k] = q
        sum_step[k] = jnp.broadcast_to(
            jnp.sum(jnp.where(eye, step, 0.0), axis=0, keepdims=True), sum_step.shape[1:]
        )
        for copy in sum_copies(k, up):
            copy.start()

    def take(k, up):
        line_copy(k, up).wait_recv()
        pass_on(k, up)
        select(k)

    def step_along(s, c):
        @pl.when(s > 0)
        def _():
            pl.when(z - s >= 0)(lambda: take(z - s, True))
            pl.when(z + s < n_z)(lambda: take(z + s, False))

        down = s - (n_z - 1 - z)
        pl.when((down >= 0) & (down < z))(lambda: relay(down, False, z == n_z - 1))
        up = n_z - 1 - s + z
        pl.when((up > z) & (up < n_z))(lambda: relay(up, True, z == 0))
        return c

    lax.fori_loop(0, n_z, step_along, 0)
    sum_mine[...] = gathered(z)

    def val_wait(k, d, h, g):
        cols_d = pl.ds(pl.multiple_of(d * cols, cols), cols)
        plane(
            picked.at[k, g], arrived.at[k * n_x + h, :, cols_d], val_ss.at[k, g], val_rs.at[k, g], d, h
        ).wait_recv()

    for k in range(n_z):
        every(lambda d, h, g: val_wait(k, d, h, g))

    def tokens(b, scores):
        at = pl.ds(pl.multiple_of(b * cols, cols), cols)
        table = arrived[:, :, at].reshape(spread, cols)
        out_ref[:, at] = lax.dot_general(
            dense_w[...], table, (((0,), (0,)), ((), ())), preferred_element_type=jnp.float32
        ).astype(out_ref.dtype)
        return scores + lax.dot_general(
            table, cot_ref[:, at], (((1,), (1,)), ((), ())), preferred_element_type=jnp.float32
        )

    scores = lax.fori_loop(0, n_dp, tokens, jnp.zeros((spread, toks), jnp.float32))
    for k in range(topk):
        wgrad_ref[k : k + 1, :] = jnp.sum(
            jnp.where(pos_ref[k : k + 1, :] == place_of, scores, 0.0), axis=0, keepdims=True
        )

    @pl.when(has_above)
    def _():
        sum_mine[...] += received(z)

    @pl.when(has_below)
    def _():
        sum_mine[...] += received(n_z)

    vgrad_ref[...] = sum_mine[...]

    every(lambda d, h, g: list_copy(d, h, g).wait_send())
    every(lambda d, h, g: step_copy(d, h, g).wait_send())

    def sent(k, c):
        every(lambda d, h, g: grad_copy(k, d, h, g).wait_send())
        every(lambda d, h, g: val_copy(k, d, h, g).wait_send())
        for up in (False, True):
            pl.when((has_above & (k <= z)) if up else (has_below & (k >= z)))(
                lambda: line_copy(k, up).wait_send()
            )

            @pl.when((k > z) if up else (k < z))
            def _():
                for copy in sum_copies(k, up):
                    copy.wait_send()
        return c

    lax.fori_loop(0, n_z, sent, 0)


def on_device(n_dp, n_mem, slot_weight, slot_pos, touched, values, cotangent):
    toks, topk = slot_pos.shape
    lists = touched[0]
    cap = lists.shape[1]
    rows, width = values.shape
    cols = width // n_dp
    n_x = 1
    while 4 * n_x * n_x <= n_mem:
        n_x *= 2
    n_z = n_mem // n_x
    group = n_dp * n_x
    f32, bf16, i16 = jnp.float32, jnp.bfloat16, jnp.int16
    dma = pltpu.SemaphoreType.DMA
    vmem = pl.BlockSpec(memory_space=pltpu.VMEM)
    out, wgrad, vgrad = pl.pallas_call(
        functools.partial(kernel, n_dp, n_mem, n_x),
        out_shape=(
            jax.ShapeDtypeStruct((toks, width), bf16),
            jax.ShapeDtypeStruct((topk, toks), f32),
            jax.ShapeDtypeStruct((rows, cols), f32),
        ),
        in_specs=[vmem, vmem, vmem, vmem, pl.BlockSpec(memory_space=pl.ANY)],
        out_specs=(vmem, vmem, vmem),
        scratch_shapes=[
            pltpu.VMEM((n_mem * cap, toks), bf16),
            pltpu.VMEM((n_dp, n_mem, cap), f32),
            pltpu.VMEM((group, n_mem, cap), f32),
            pltpu.VMEM((group, n_mem, cap), jnp.int32),
            pltpu.VMEM((n_dp, n_mem, cap, cols), i16),
            pltpu.VMEM((n_z, group, cap, cols), i16),
            pltpu.VMEM((n_z, rows, group * cap), bf16),
            pltpu.VMEM((n_z, rows, cols), bf16),
            pltpu.VMEM((n_z, group, cap, cols), bf16),
            pltpu.VMEM((n_mem, cap, width), bf16),
            pltpu.VMEM((rows, cols), f32),
            pltpu.VMEM((n_z, rows, cols), i16),
            pltpu.VMEM((n_z + 1, rows, cols), i16),
            pltpu.VMEM((n_z, 8, rows), f32),
            pltpu.VMEM((n_z + 1, 8, rows), f32),
            dma((group,)), dma((group,)),
            dma((group,)), dma((group,)),
            dma((n_z, group)), dma((n_z, group)),
            dma((n_z, group)), dma((n_z, group)),
            dma((2, n_z)), dma((n_z,)),
            dma((2, n_z)), dma((2, n_z + 1)),
            dma,
        ],
        compiler_params=pltpu.CompilerParams(
            collective_id=0, has_side_effects=True, vmem_limit_bytes=60 * 2**20
        ),
    )(lists, slot_pos.T, slot_weight.T, cotangent, values)
    return out, wgrad.T, vgrad


def solution(mesh):
    return jax.shard_map(
        functools.partial(on_device, mesh.shape["dp"], mesh.shape["mem"]),
        mesh=mesh,
        in_specs=(
            P(("dp", "mem"), None),
            P(("dp", "mem"), None),
            P(("dp", "mem"), None, None),
            P("mem", None),
            P(("dp", "mem"), None),
        ),
        out_specs=(P(("dp", "mem"), None), P(("dp", "mem"), None), P("mem", "dp")),
        check_vma=False,
    )
```

```python
import functools

import jax
import jax.numpy as jnp
from jax import lax
from jax.experimental import pallas as pl
from jax.experimental.pallas import tpu as pltpu
from jax.sharding import PartitionSpec as P

MESH = pl.DeviceIdType.MESH
STEPS = 32000.0
CHUNKS = 2


def iota(shape, axis):
    return lax.broadcasted_iota(jnp.int32, shape, axis)


def coded(x):
    top = jnp.max(jnp.abs(x), axis=1, keepdims=True)
    step = jnp.maximum(top * (1.0 / STEPS), 1e-30).astype(jnp.bfloat16).astype(jnp.float32)
    return jnp.round(x * (1.0 / step)).astype(jnp.int32).astype(jnp.int16), step


def pieces(q):
    full = q.astype(jnp.int32).astype(jnp.float32)
    high = full.astype(jnp.bfloat16)
    return high, (full - high.astype(jnp.float32)).astype(jnp.bfloat16)


def decoded_sum(hot, q):
    high, low = pieces(q)
    return jnp.dot(hot, high, preferred_element_type=jnp.float32) + jnp.dot(
        hot, low, preferred_element_type=jnp.float32
    )


def kernel(
    n_dp, n_mem, n_x,
    lists_ref, pos_ref, w_ref, cot_ref, values_ref,
    out_ref, wgrad_ref, vgrad_ref,
    dense_w, step_mine, step_got, lists_got, coded_mine, coded_got, hot, vals, picked, arrived,
    sum_mine, sum_part, sum_coded, sum_got, sum_step, sum_step_got,
    list_ss, list_rs, step_ss, step_rs, grad_ss, grad_rs, val_ss, val_rs,
    line_ss, line_rs, sum_ss, sum_rs, own_sem,
):
    n_z = n_mem // n_x
    group = n_dp * n_x
    cap = lists_ref.shape[1]
    topk, toks = pos_ref.shape
    rows = values_ref.shape[0]
    cols = cot_ref.shape[1] // n_dp
    spread = n_mem * cap
    bits = cap.bit_length() - 1
    dp = lax.axis_index("dp")
    mem = lax.axis_index("mem")
    z = mem // n_x
    x = lax.rem(mem, n_x)
    me = dp * n_x + x
    has_below, has_above = z > 0, z < n_z - 1

    def place(t):
        d = lax.rem(dp + 1 + t // n_x, n_dp)
        h = lax.rem(x + 1 + lax.rem(t, n_x), n_x)
        return d, h, d * n_x + h

    def every(fn):
        def body(t, c):
            fn(*place(t))
            return c
        lax.fori_loop(0, group - 1, body, 0)

    def remote(src, dst, ss, rs, d, m):
        return pltpu.make_async_remote_copy(
            src_ref=src, dst_ref=dst, send_sem=ss, recv_sem=rs, device_id=(d, m), device_id_type=MESH
        )

    def plane(src, dst, ss, rs, d, h):
        return remote(src, dst, ss, rs, d, z * n_x + h)

    barrier = pltpu.get_barrier_semaphore()

    def greet(m):
        pl.semaphore_signal(barrier, inc=1, device_id=(dp, m), device_id_type=MESH)

    every(
        lambda d, h, g: pl.semaphore_signal(
            barrier, inc=1, device_id=(d, z * n_x + h), device_id_type=MESH
        )
    )
    pl.when(has_below)(lambda: greet(mem - n_x))
    pl.when(has_above)(lambda: greet(mem + n_x))

    my_cols = pl.ds(pl.multiple_of(dp * cols, cols), cols)
    own = pltpu.make_async_copy(values_ref.at[:, my_cols], vals.at[z], own_sem)
    own.start()
    lists_got[me] = lists_ref[...]

    place_of = iota((spread, toks), 0)
    acc = jnp.zeros((spread, toks), jnp.float32)
    weights = w_ref[...].astype(jnp.float32)
    for k in range(topk):
        acc = jnp.where(pos_ref[k : k + 1, :] == place_of, weights[k : k + 1, :], acc)
    dense_w[...] = acc.astype(jnp.bfloat16)

    pl.semaphore_wait(barrier, group - 1 + has_below.astype(jnp.int32) + has_above.astype(jnp.int32))

    wide = cols // CHUNKS

    def line_copy(k, up, c):
        way = 1 if up else 0
        part = vals.at[k, :, pl.ds(c * wide, wide)]
        to = mem + n_x if up else mem - n_x
        return remote(part, part, line_ss.at[way, c, k], line_rs.at[c, k], dp, to)

    def pass_on(k, up, c):
        pl.when(has_above if up else has_below)(lambda: line_copy(k, up, c).start())

    def list_copy(d, h, g):
        return plane(lists_ref, lists_got.at[me], list_ss.at[g], list_rs.at[me], d, h)

    every(lambda d, h, g: list_copy(d, h, g).start())
    own.wait()
    for c in range(CHUNKS):
        pass_on(z, True, c)
        pass_on(z, False, c)

    def grad_copy(k, d, h, g):
        return plane(
            coded_mine.at[d, k * n_x + h], coded_got.at[k, me], grad_ss.at[k, g], grad_rs.at[k, me], d, h
        )

    def step_copy(d, h, g):
        return plane(step_mine.at[d], step_got.at[me], step_ss.at[g], step_rs.at[me], d, h)

    to_owner = (iota((n_mem, spread), 1) >> bits == iota((n_mem, spread), 0)).astype(jnp.bfloat16)
    to_lane = iota((spread, cap), 0) & (cap - 1) == iota((spread, cap), 1)

    def terms_of(d, c):
        block = cot_ref[:, pl.ds(pl.multiple_of(d * cols, cols), cols)]
        q, step = coded(jnp.dot(dense_w[...], block, preferred_element_type=jnp.float32))
        coded_mine[d] = q.reshape(n_mem, cap, cols)
        step_mine[d] = jnp.dot(
            to_owner, jnp.where(to_lane, step, 0.0).astype(jnp.bfloat16), preferred_element_type=jnp.float32
        )
        return c

    lax.fori_loop(0, n_dp, terms_of, 0)
    every(lambda d, h, g: step_copy(d, h, g).start())
    for i in range(n_z):
        k = jnp.where(z >= n_z // 2, i, n_z - 1 - i)
        every(lambda d, h, g: grad_copy(k, d, h, g).start())
        coded_got[k, me] = coded_mine[dp, k * n_x + x]
    step_got[me] = step_mine[dp]

    every(lambda d, h, g: plane(lists_ref, lists_got.at[g], list_ss.at[g], list_rs.at[g], d, h).wait_recv())
    slots = group * cap
    fan = (iota((cap, slots), 1) & (cap - 1) == iota((cap, slots), 0)).astype(jnp.bfloat16)
    diag = iota((group, slots), 1) >> bits == iota((group, slots), 0)

    def along_lanes(table, m):
        pick = iota(table.shape, 1) == m
        part = jnp.sum(jnp.where(pick, table, 0.0), axis=1).astype(jnp.bfloat16)
        wide = jnp.dot(part, fan, preferred_element_type=jnp.float32)
        return jnp.sum(jnp.where(diag, wide, 0.0), axis=0, keepdims=True)

    row_of = iota((rows, slots), 0).astype(jnp.float32)

    def hot_of(k, c):
        lists_f = lists_got[...].astype(jnp.float32)
        hot[k] = (row_of == along_lanes(lists_f, k * n_x + x)).astype(jnp.bfloat16)
        return c

    lax.fori_loop(0, n_z, hot_of, 0)

    def val_copy(k, d, h, g):
        return plane(
            picked.at[k, g], arrived.at[k * n_x + x, :, my_cols], val_ss.at[k, g], val_rs.at[k, me], d, h
        )

    def select(k):
        got = lax.dot_general(
            hot[k], vals[k], (((0,), (0,)), ((), ())), preferred_element_type=jnp.float32
        )
        picked[k] = got.astype(jnp.bfloat16).reshape(group, cap, cols)
        every(lambda d, h, g: val_copy(k, d, h, g).start())
        arrived[k * n_x + x, :, my_cols] = picked[k, me]

    select(z)

    every(
        lambda d, h, g: plane(step_mine.at[0], step_got.at[g], step_ss.at[g], step_rs.at[g], d, h).wait_recv()
    )
    eye = iota((rows, rows), 0) == iota((rows, rows), 1)

    def gather_wait(k):
        every(
            lambda d, h, g: plane(
                coded_mine.at[0, 0], coded_got.at[k, g], grad_ss.at[k, g], grad_rs.at[k, g], d, h
            ).wait_recv()
        )

    def scaled_hot(k):
        return (hot[k].astype(jnp.float32) * along_lanes(step_got[...], k * n_x + x)).astype(jnp.bfloat16)

    def gathered(k, scaled, c):
        return decoded_sum(scaled, coded_got[k, :, :, c * wide : (c + 1) * wide].reshape(slots, wide))

    def sum_copies(k, up, c):
        to = mem + n_x if up else mem - n_x
        at = jnp.where(k == z + 1, n_z, k) if up else k
        return (
            remote(sum_step.at[c, k], sum_step_got.at[c, at], sum_ss.at[0, c, k], sum_rs.at[0, c, at], dp, to),
            remote(sum_coded.at[c, k], sum_got.at[c, at], sum_ss.at[1, c, k], sum_rs.at[1, c, at], dp, to),
        )

    def received(at, c):
        for src, dst, i in ((sum_step, sum_step_got, 0), (sum_coded, sum_got, 1)):
            remote(src.at[c, 0], dst.at[c, at], sum_ss.at[i, c, 0], sum_rs.at[i, c, at], dp, mem).wait_recv()
        scaled = jnp.where(eye, sum_step_got[c, at][0:1, :], 0.0).astype(jnp.bfloat16)
        return decoded_sum(scaled, sum_got[c, at])

    def relay(k, up, first):
        gather_wait(k)
        scaled = scaled_hot(k)
        for c in range(CHUNKS):
            sum_part[...] = gathered(k, scaled, c)

            @pl.when(jnp.logical_not(first))
            def _():
                sum_part[...] += received(k, c)

            q, step = coded(sum_part[...])
            sum_coded[c, k] = q
            sum_step[c, k] = jnp.broadcast_to(
                jnp.sum(jnp.where(eye, step, 0.0), axis=0, keepdims=True), sum_step.shape[2:]
            )
            for copy in sum_copies(k, up, c):
                copy.start()

    def take(k, up, c):
        line_copy(k, up, c).wait_recv()
        pass_on(k, up, c)

    def step_along(s, carry):
        @pl.when(s > 0)
        def _():
            from_below, from_above = z - s >= 0, z + s < n_z
            for c in range(CHUNKS):
                pl.when(from_below)(lambda: take(z - s, True, c))
                pl.when(from_above)(lambda: take(z + s, False, c))
            pl.when(from_below)(lambda: select(z - s))
            pl.when(from_above)(lambda: select(z + s))

        down = s - (n_z - 1 - z)
        pl.when((down >= 0) & (down < z))(lambda: relay(down, False, z == n_z - 1))
        up = n_z - 1 - s + z
        pl.when((up > z) & (up < n_z))(lambda: relay(up, True, z == 0))
        return carry

    lax.fori_loop(0, n_z, step_along, 0)
    gather_wait(z)
    own_hot = scaled_hot(z)
    for c in range(CHUNKS):
        sum_mine[:, c * wide : (c + 1) * wide] = gathered(z, own_hot, c)

    def val_wait(k, d, h, g):
        cols_d = pl.ds(pl.multiple_of(d * cols, cols), cols)
        plane(
            picked.at[k, g], arrived.at[k * n_x + h, :, cols_d], val_ss.at[k, g], val_rs.at[k, g], d, h
        ).wait_recv()

    for k in range(n_z):
        every(lambda d, h, g: val_wait(k, d, h, g))

    def tokens(b, scores):
        at = pl.ds(pl.multiple_of(b * cols, cols), cols)
        table = arrived[:, :, at].reshape(spread, cols)
        out_ref[:, at] = lax.dot_general(
            dense_w[...], table, (((0,), (0,)), ((), ())), preferred_element_type=jnp.float32
        ).astype(out_ref.dtype)
        return scores + lax.dot_general(
            table, cot_ref[:, at], (((1,), (1,)), ((), ())), preferred_element_type=jnp.float32
        )

    scores = lax.fori_loop(0, n_dp, tokens, jnp.zeros((spread, toks), jnp.float32))
    for k in range(topk):
        wgrad_ref[k : k + 1, :] = jnp.sum(
            jnp.where(pos_ref[k : k + 1, :] == place_of, scores, 0.0), axis=0, keepdims=True
        )

    every(lambda d, h, g: list_copy(d, h, g).wait_send())
    every(lambda d, h, g: step_copy(d, h, g).wait_send())

    def sent(k, carry):
        every(lambda d, h, g: grad_copy(k, d, h, g).wait_send())
        every(lambda d, h, g: val_copy(k, d, h, g).wait_send())
        for up in (False, True):
            @pl.when((has_above & (k <= z)) if up else (has_below & (k >= z)))
            def _():
                for c in range(CHUNKS):
                    line_copy(k, up, c).wait_send()
        return carry

    lax.fori_loop(0, n_z, sent, 0)

    for c in range(CHUNKS):
        at = slice(c * wide, (c + 1) * wide)

        @pl.when(has_above)
        def _():
            sum_mine[:, at] += received(z, c)

        @pl.when(has_below)
        def _():
            sum_mine[:, at] += received(n_z, c)

        vgrad_ref[:, at] = sum_mine[:, at]

    def sums_sent(k, carry):
        for up in (False, True):
            @pl.when((k > z) if up else (k < z))
            def _():
                for c in range(CHUNKS):
                    for copy in sum_copies(k, up, c):
                        copy.wait_send()
        return carry

    lax.fori_loop(0, n_z, sums_sent, 0)


def on_device(n_dp, n_mem, slot_weight, slot_pos, touched, values, cotangent):
    toks, topk = slot_pos.shape
    lists = touched[0]
    cap = lists.shape[1]
    rows, width = values.shape
    cols = width // n_dp
    n_x = 1
    while 4 * n_x * n_x <= n_mem:
        n_x *= 2
    n_z = n_mem // n_x
    group = n_dp * n_x
    f32, bf16, i16 = jnp.float32, jnp.bfloat16, jnp.int16
    dma = pltpu.SemaphoreType.DMA
    vmem = pl.BlockSpec(memory_space=pltpu.VMEM)
    out, wgrad, vgrad = pl.pallas_call(
        functools.partial(kernel, n_dp, n_mem, n_x),
        out_shape=(
            jax.ShapeDtypeStruct((toks, width), bf16),
            jax.ShapeDtypeStruct((topk, toks), f32),
            jax.ShapeDtypeStruct((rows, cols), f32),
        ),
        in_specs=[vmem, vmem, vmem, vmem, pl.BlockSpec(memory_space=pl.ANY)],
        out_specs=(vmem, vmem, vmem),
        scratch_shapes=[
            pltpu.VMEM((n_mem * cap, toks), bf16),
            pltpu.VMEM((n_dp, n_mem, cap), f32),
            pltpu.VMEM((group, n_mem, cap), f32),
            pltpu.VMEM((group, n_mem, cap), jnp.int32),
            pltpu.VMEM((n_dp, n_mem, cap, cols), i16),
            pltpu.VMEM((n_z, group, cap, cols), i16),
            pltpu.VMEM((n_z, rows, group * cap), bf16),
            pltpu.VMEM((n_z, rows, cols), bf16),
            pltpu.VMEM((n_z, group, cap, cols), bf16),
            pltpu.VMEM((n_mem, cap, width), bf16),
            pltpu.VMEM((rows, cols), f32),
            pltpu.VMEM((rows, cols // CHUNKS), f32),
            pltpu.VMEM((CHUNKS, n_z, rows, cols // CHUNKS), i16),
            pltpu.VMEM((CHUNKS, n_z + 1, rows, cols // CHUNKS), i16),
            pltpu.VMEM((CHUNKS, n_z, 8, rows), f32),
            pltpu.VMEM((CHUNKS, n_z + 1, 8, rows), f32),
            dma((group,)), dma((group,)),
            dma((group,)), dma((group,)),
            dma((n_z, group)), dma((n_z, group)),
            dma((n_z, group)), dma((n_z, group)),
            dma((2, CHUNKS, n_z)), dma((CHUNKS, n_z)),
            dma((2, CHUNKS, n_z)), dma((2, CHUNKS, n_z + 1)),
            dma,
        ],
        compiler_params=pltpu.CompilerParams(
            collective_id=0, has_side_effects=True, vmem_limit_bytes=60 * 2**20
        ),
    )(lists, slot_pos.T, slot_weight.T, cotangent, values)
    return out, wgrad.T, vgrad


def solution(mesh):
    return jax.shard_map(
        functools.partial(on_device, mesh.shape["dp"], mesh.shape["mem"]),
        mesh=mesh,
        in_specs=(
            P(("dp", "mem"), None),
            P(("dp", "mem"), None),
            P(("dp", "mem"), None, None),
            P("mem", None),
            P(("dp", "mem"), None),
        ),
        out_specs=(P(("dp", "mem"), None), P(("dp", "mem"), None), P("mem", "dp")),
        check_vma=False,
    )
```

```python
import functools

import jax
import jax.numpy as jnp
from jax import lax
from jax.experimental import pallas as pl
from jax.experimental.pallas import tpu as pltpu
from jax.sharding import PartitionSpec as P

MESH = pl.DeviceIdType.MESH
STEPS = 32000.0
CHUNKS = 2


def iota(shape, axis):
    return lax.broadcasted_iota(jnp.int32, shape, axis)


def coded(x):
    top = jnp.max(jnp.abs(x), axis=1, keepdims=True)
    step = jnp.maximum(top * (1.0 / STEPS), 1e-30).astype(jnp.bfloat16).astype(jnp.float32)
    return jnp.round(x * (1.0 / step)).astype(jnp.int32).astype(jnp.int16), step


def pieces(q):
    full = q.astype(jnp.int32).astype(jnp.float32)
    high = full.astype(jnp.bfloat16)
    return high, (full - high.astype(jnp.float32)).astype(jnp.bfloat16)


def decoded_sum(hot, q):
    high, low = pieces(q)
    return jnp.dot(hot, high, preferred_element_type=jnp.float32) + jnp.dot(
        hot, low, preferred_element_type=jnp.float32
    )


def kernel(
    n_dp, n_mem, n_x,
    lists_ref, pos_ref, w_ref, cot_ref, values_ref,
    out_ref, wgrad_ref, vgrad_ref,
    dense_w, step_mine, step_got, lists_got, coded_mine, coded_got, hot, vals, picked, arrived,
    sum_mine, sum_part, sum_coded, sum_got, sum_step, sum_step_got,
    list_ss, list_rs, step_ss, step_rs, grad_ss, grad_rs, val_ss, val_rs,
    line_ss, line_rs, sum_ss, sum_rs, own_sem,
):
    n_z = n_mem // n_x
    group = n_dp * n_x
    cap = lists_ref.shape[1]
    topk, toks = pos_ref.shape
    rows = values_ref.shape[0]
    cols = cot_ref.shape[1] // n_dp
    spread = n_mem * cap
    bits = cap.bit_length() - 1
    dp = lax.axis_index("dp")
    mem = lax.axis_index("mem")
    z = mem // n_x
    x = lax.rem(mem, n_x)
    me = dp * n_x + x
    has_below, has_above = z > 0, z < n_z - 1

    def place(t):
        d = lax.rem(dp + 1 + t // n_x, n_dp)
        h = lax.rem(x + 1 + lax.rem(t, n_x), n_x)
        return d, h, d * n_x + h

    places = [place(t) for t in range(group - 1)] if group <= 8 else None

    def every(fn):
        if places is not None:
            for spot in places:
                fn(*spot)
            return

        def body(t, c):
            fn(*place(t))
            return c
        lax.fori_loop(0, group - 1, body, 0)

    def all_sent(like, sem):
        plane(like, like, sem, sem, dp, x).wait_send()

    def all_here(like, sem):
        plane(like, like, sem, sem, dp, x).wait_recv()

    def remote(src, dst, ss, rs, d, m):
        return pltpu.make_async_remote_copy(
            src_ref=src, dst_ref=dst, send_sem=ss, recv_sem=rs, device_id=(d, m), device_id_type=MESH
        )

    def plane(src, dst, ss, rs, d, h):
        return remote(src, dst, ss, rs, d, z * n_x + h)

    barrier = pltpu.get_barrier_semaphore()

    def greet(m):
        pl.semaphore_signal(barrier, inc=1, device_id=(dp, m), device_id_type=MESH)

    every(
        lambda d, h, g: pl.semaphore_signal(
            barrier, inc=1, device_id=(d, z * n_x + h), device_id_type=MESH
        )
    )
    pl.when(has_below)(lambda: greet(mem - n_x))
    pl.when(has_above)(lambda: greet(mem + n_x))

    my_cols = pl.ds(pl.multiple_of(dp * cols, cols), cols)
    own = pltpu.make_async_copy(values_ref.at[:, my_cols], vals.at[z], own_sem)
    own.start()
    lists_got[me] = lists_ref[...]

    place_of = iota((spread, toks), 0)
    acc = jnp.zeros((spread, toks), jnp.float32)
    weights = w_ref[...].astype(jnp.float32)
    for k in range(topk):
        acc = jnp.where(pos_ref[k : k + 1, :] == place_of, weights[k : k + 1, :], acc)
    dense_w[...] = acc.astype(jnp.bfloat16)

    pl.semaphore_wait(barrier, group - 1 + has_below.astype(jnp.int32) + has_above.astype(jnp.int32))

    wide = cols // CHUNKS

    def line_copy(k, up, c):
        way = 1 if up else 0
        part = vals.at[k, :, pl.ds(c * wide, wide)]
        to = mem + n_x if up else mem - n_x
        return remote(part, part, line_ss.at[way, c, k], line_rs.at[c, k], dp, to)

    def pass_on(k, up, c):
        pl.when(has_above if up else has_below)(lambda: line_copy(k, up, c).start())

    def list_copy(d, h, g):
        return plane(lists_ref, lists_got.at[me], list_ss.at[0], list_rs.at[0], d, h)

    every(lambda d, h, g: list_copy(d, h, g).start())
    own.wait()
    for c in range(CHUNKS):
        pass_on(z, True, c)
        pass_on(z, False, c)

    def grad_copy(k, d, h, g):
        return plane(
            coded_mine.at[k, d, h], coded_got.at[k, me], grad_ss.at[k], grad_rs.at[k], d, h
        )

    def step_copy(d, h, g):
        return plane(step_mine.at[d], step_got.at[me], step_ss.at[0], step_rs.at[0], d, h)

    part = n_x * cap
    to_lane = iota((part, cap), 0) & (cap - 1) == iota((part, cap), 1)
    steps = [jnp.zeros((n_mem, cap), jnp.float32) for _ in range(n_dp)]
    for i in range(n_z):
        k = jnp.where(z >= n_z // 2, i, n_z - 1 - i)
        weights_k = dense_w[pl.ds(pl.multiple_of(k * part, part), part), :]
        to_owner = iota((n_mem, part), 0) == (iota((n_mem, part), 1) >> bits) + k * n_x
        for d in range(n_dp):
            q, step = coded(
                jnp.dot(weights_k, cot_ref[:, d * cols : (d + 1) * cols], preferred_element_type=jnp.float32)
            )
            coded_mine[k, d] = q.reshape(n_x, cap, cols)
            steps[d] += jnp.dot(
                to_owner.astype(jnp.bfloat16),
                jnp.where(to_lane, step, 0.0).astype(jnp.bfloat16),
                preferred_element_type=jnp.float32,
            )
        every(lambda d, h, g: grad_copy(k, d, h, g).start())
    for d in range(n_dp):
        step_mine[d] = steps[d]
    every(lambda d, h, g: step_copy(d, h, g).start())
    step_got[me] = step_mine[dp]
    for k in range(n_z):
        coded_got[k, me] = coded_mine[k, dp, x]

    others = pl.ds(0, group - 1)
    all_here(lists_got.at[others], list_rs.at[0])
    slots = group * cap
    fan = (iota((cap, slots), 1) & (cap - 1) == iota((cap, slots), 0)).astype(jnp.bfloat16)
    diag = iota((group, slots), 1) >> bits == iota((group, slots), 0)

    def along_lanes(table, m):
        pick = iota(table.shape, 1) == m
        part = jnp.sum(jnp.where(pick, table, 0.0), axis=1).astype(jnp.bfloat16)
        wide = jnp.dot(part, fan, preferred_element_type=jnp.float32)
        return jnp.sum(jnp.where(diag, wide, 0.0), axis=0, keepdims=True)

    row_of = iota((rows, slots), 0).astype(jnp.float32)

    def hot_of(k, c):
        lists_f = lists_got[...].astype(jnp.float32)
        hot[k] = (row_of == along_lanes(lists_f, k * n_x + x)).astype(jnp.bfloat16)
        return c

    lax.fori_loop(0, n_z, hot_of, 0)

    def val_copy(k, d, h, g):
        return plane(
            picked.at[k, g], arrived.at[k * n_x + x, :, my_cols], val_ss.at[k], val_rs.at[k], d, h
        )

    def select(k):
        got = lax.dot_general(
            hot[k], vals[k], (((0,), (0,)), ((), ())), preferred_element_type=jnp.float32
        )
        picked[k] = got.astype(jnp.bfloat16).reshape(group, cap, cols)
        every(lambda d, h, g: val_copy(k, d, h, g).start())
        arrived[k * n_x + x, :, my_cols] = picked[k, me]

    select(z)

    all_here(step_got.at[others], step_rs.at[0])
    eye = iota((rows, rows), 0) == iota((rows, rows), 1)

    def gather_wait(k):
        all_here(coded_got.at[k, others], grad_rs.at[k])

    def scaled_hot(k):
        return (hot[k].astype(jnp.float32) * along_lanes(step_got[...], k * n_x + x)).astype(jnp.bfloat16)

    def gathered(k, scaled, c):
        return decoded_sum(scaled, coded_got[k, :, :, c * wide : (c + 1) * wide].reshape(slots, wide))

    def sum_copies(k, up, c):
        to = mem + n_x if up else mem - n_x
        at = jnp.where(k == z + 1, n_z, k) if up else k
        return (
            remote(sum_step.at[c, k], sum_step_got.at[c, at], sum_ss.at[0, c, k], sum_rs.at[0, c, at], dp, to),
            remote(sum_coded.at[c, k], sum_got.at[c, at], sum_ss.at[1, c, k], sum_rs.at[1, c, at], dp, to),
        )

    def received(at, c):
        for src, dst, i in ((sum_step, sum_step_got, 0), (sum_coded, sum_got, 1)):
            remote(src.at[c, 0], dst.at[c, at], sum_ss.at[i, c, 0], sum_rs.at[i, c, at], dp, mem).wait_recv()
        scaled = jnp.where(eye, sum_step_got[c, at][0:1, :], 0.0).astype(jnp.bfloat16)
        return decoded_sum(scaled, sum_got[c, at])

    def relay(k, up, first):
        gather_wait(k)
        scaled = scaled_hot(k)
        for c in range(CHUNKS):
            sum_part[...] = gathered(k, scaled, c)

            @pl.when(jnp.logical_not(first))
            def _():
                sum_part[...] += received(k, c)

            q, step = coded(sum_part[...])
            sum_coded[c, k] = q
            sum_step[c, k] = jnp.broadcast_to(
                jnp.sum(jnp.where(eye, step, 0.0), axis=0, keepdims=True), sum_step.shape[2:]
            )
            for copy in sum_copies(k, up, c):
                copy.start()

    def take(k, up, c):
        line_copy(k, up, c).wait_recv()
        pass_on(k, up, c)

    def step_along(s, carry):
        @pl.when(s > 0)
        def _():
            from_below, from_above = z - s >= 0, z + s < n_z
            for c in range(CHUNKS):
                pl.when(from_below)(lambda: take(z - s, True, c))
                pl.when(from_above)(lambda: take(z + s, False, c))
            pl.when(from_below)(lambda: select(z - s))
            pl.when(from_above)(lambda: select(z + s))

        down = s - (n_z - 1 - z)
        pl.when((down >= 0) & (down < z))(lambda: relay(down, False, z == n_z - 1))
        up = n_z - 1 - s + z
        pl.when((up > z) & (up < n_z))(lambda: relay(up, True, z == 0))
        return carry

    lax.fori_loop(0, n_z, step_along, 0)
    gather_wait(z)
    own_hot = scaled_hot(z)
    for c in range(CHUNKS):
        sum_mine[:, c * wide : (c + 1) * wide] = gathered(z, own_hot, c)

    for k in range(n_z):
        all_here(picked.at[k, others], val_rs.at[k])

    def tokens(b, scores):
        at = pl.ds(pl.multiple_of(b * cols, cols), cols)
        table = arrived[:, :, at].reshape(spread, cols)
        out_ref[:, at] = lax.dot_general(
            dense_w[...], table, (((0,), (0,)), ((), ())), preferred_element_type=jnp.float32
        ).astype(out_ref.dtype)
        return scores + lax.dot_general(
            table, cot_ref[:, at], (((1,), (1,)), ((), ())), preferred_element_type=jnp.float32
        )

    scores = lax.fori_loop(0, n_dp, tokens, jnp.zeros((spread, toks), jnp.float32))
    for k in range(topk):
        wgrad_ref[k : k + 1, :] = jnp.sum(
            jnp.where(pos_ref[k : k + 1, :] == place_of, scores, 0.0), axis=0, keepdims=True
        )

    all_sent(lists_got.at[others], list_ss.at[0])
    all_sent(step_got.at[others], step_ss.at[0])

    def sent(k, carry):
        all_sent(coded_got.at[k, others], grad_ss.at[k])
        all_sent(picked.at[k, others], val_ss.at[k])
        for up in (False, True):
            @pl.when((has_above & (k <= z)) if up else (has_below & (k >= z)))
            def _():
                for c in range(CHUNKS):
                    line_copy(k, up, c).wait_send()
        return carry

    lax.fori_loop(0, n_z, sent, 0)

    for c in range(CHUNKS):
        at = slice(c * wide, (c + 1) * wide)

        @pl.when(has_above)
        def _():
            sum_mine[:, at] += received(z, c)

        @pl.when(has_below)
        def _():
            sum_mine[:, at] += received(n_z, c)

        vgrad_ref[:, at] = sum_mine[:, at]

    def sums_sent(k, carry):
        for up in (False, True):
            @pl.when((k > z) if up else (k < z))
            def _():
                for c in range(CHUNKS):
                    for copy in sum_copies(k, up, c):
                        copy.wait_send()
        return carry

    lax.fori_loop(0, n_z, sums_sent, 0)


def on_device(n_dp, n_mem, slot_weight, slot_pos, touched, values, cotangent):
    toks, topk = slot_pos.shape
    lists = touched[0]
    cap = lists.shape[1]
    rows, width = values.shape
    cols = width // n_dp
    n_x = 1
    while 4 * n_x * n_x <= n_mem:
        n_x *= 2
    n_z = n_mem // n_x
    group = n_dp * n_x
    f32, bf16, i16 = jnp.float32, jnp.bfloat16, jnp.int16
    dma = pltpu.SemaphoreType.DMA
    vmem = pl.BlockSpec(memory_space=pltpu.VMEM)
    out, wgrad, vgrad = pl.pallas_call(
        functools.partial(kernel, n_dp, n_mem, n_x),
        out_shape=(
            jax.ShapeDtypeStruct((toks, width), bf16),
            jax.ShapeDtypeStruct((topk, toks), f32),
            jax.ShapeDtypeStruct((rows, cols), f32),
        ),
        in_specs=[vmem, vmem, vmem, vmem, pl.BlockSpec(memory_space=pl.ANY)],
        out_specs=(vmem, vmem, vmem),
        scratch_shapes=[
            pltpu.VMEM((n_mem * cap, toks), bf16),
            pltpu.VMEM((n_dp, n_mem, cap), f32),
            pltpu.VMEM((group, n_mem, cap), f32),
            pltpu.VMEM((group, n_mem, cap), jnp.int32),
            pltpu.VMEM((n_z, n_dp, n_x, cap, cols), i16),
            pltpu.VMEM((n_z, group, cap, cols), i16),
            pltpu.VMEM((n_z, rows, group * cap), bf16),
            pltpu.VMEM((n_z, rows, cols), bf16),
            pltpu.VMEM((n_z, group, cap, cols), bf16),
            pltpu.VMEM((n_mem, cap, width), bf16),
            pltpu.VMEM((rows, cols), f32),
            pltpu.VMEM((rows, cols // CHUNKS), f32),
            pltpu.VMEM((CHUNKS, n_z, rows, cols // CHUNKS), i16),
            pltpu.VMEM((CHUNKS, n_z + 1, rows, cols // CHUNKS), i16),
            pltpu.VMEM((CHUNKS, n_z, 8, rows), f32),
            pltpu.VMEM((CHUNKS, n_z + 1, 8, rows), f32),
            dma((1,)), dma((1,)),
            dma((1,)), dma((1,)),
            dma((n_z,)), dma((n_z,)),
            dma((n_z,)), dma((n_z,)),
            dma((2, CHUNKS, n_z)), dma((CHUNKS, n_z)),
            dma((2, CHUNKS, n_z)), dma((2, CHUNKS, n_z + 1)),
            dma,
        ],
        compiler_params=pltpu.CompilerParams(
            collective_id=0, has_side_effects=True, vmem_limit_bytes=60 * 2**20
        ),
    )(lists, slot_pos.T, slot_weight.T, cotangent, values)
    return out, wgrad.T, vgrad


def solution(mesh):
    return jax.shard_map(
        functools.partial(on_device, mesh.shape["dp"], mesh.shape["mem"]),
        mesh=mesh,
        in_specs=(
            P(("dp", "mem"), None),
            P(("dp", "mem"), None),
            P(("dp", "mem"), None, None),
            P("mem", None),
            P(("dp", "mem"), None),
        ),
        out_specs=(P(("dp", "mem"), None), P(("dp", "mem"), None), P("mem", "dp")),
        check_vma=False,
    )
```

```python
import functools

import jax
import jax.numpy as jnp
from jax import lax
from jax.experimental import pallas as pl
from jax.experimental.pallas import tpu as pltpu
from jax.sharding import PartitionSpec as P

MESH = pl.DeviceIdType.MESH
STEPS = 32000.0
CHUNKS = 2


def iota(shape, axis):
    return lax.broadcasted_iota(jnp.int32, shape, axis)


def coded(x):
    top = jnp.max(jnp.abs(x), axis=1, keepdims=True)
    step = jnp.maximum(top * (1.0 / STEPS), 1e-30).astype(jnp.bfloat16).astype(jnp.float32)
    return jnp.round(x * (1.0 / step)).astype(jnp.int32).astype(jnp.int16), step


def pieces(q):
    full = q.astype(jnp.int32).astype(jnp.float32)
    high = full.astype(jnp.bfloat16)
    return high, (full - high.astype(jnp.float32)).astype(jnp.bfloat16)


def decoded_sum(hot, q):
    high, low = pieces(q)
    return jnp.dot(hot, high, preferred_element_type=jnp.float32) + jnp.dot(
        hot, low, preferred_element_type=jnp.float32
    )


def kernel(
    n_dp, n_mem, n_x,
    lists_ref, pos_ref, w_ref, cot_ref, values_ref,
    out_ref, wgrad_ref, vgrad_ref,
    dense_w, step_mine, step_got, lists_got, coded_mine, coded_got, hot, vals, picked, arrived,
    sum_mine, sum_part, sum_coded, sum_got, sum_step, sum_step_got,
    list_ss, list_rs, step_ss, step_rs, grad_ss, grad_rs, val_ss, val_rs,
    line_ss, line_rs, sum_ss, sum_rs, own_sem,
):
    n_z = n_mem // n_x
    group = n_dp * n_x
    cap = lists_ref.shape[1]
    topk, toks = pos_ref.shape
    rows = values_ref.shape[0]
    cols = cot_ref.shape[1] // n_dp
    spread = n_mem * cap
    bits = cap.bit_length() - 1
    dp = lax.axis_index("dp")
    mem = lax.axis_index("mem")
    z = mem // n_x
    x = lax.rem(mem, n_x)
    me = dp * n_x + x
    has_below, has_above = z > 0, z < n_z - 1

    def place(t):
        d = lax.rem(dp + 1 + t // n_x, n_dp)
        h = lax.rem(x + 1 + lax.rem(t, n_x), n_x)
        return d, h, d * n_x + h

    places = [place(t) for t in range(group - 1)] if group <= 8 else None

    def every(fn):
        if places is not None:
            for spot in places:
                fn(*spot)
            return

        def body(t, c):
            fn(*place(t))
            return c
        lax.fori_loop(0, group - 1, body, 0)

    def all_sent(like, sem):
        plane(like, like, sem, sem, dp, x).wait_send()

    def all_here(like, sem):
        plane(like, like, sem, sem, dp, x).wait_recv()

    def remote(src, dst, ss, rs, d, m):
        return pltpu.make_async_remote_copy(
            src_ref=src, dst_ref=dst, send_sem=ss, recv_sem=rs, device_id=(d, m), device_id_type=MESH
        )

    def plane(src, dst, ss, rs, d, h):
        return remote(src, dst, ss, rs, d, z * n_x + h)

    barrier = pltpu.get_barrier_semaphore()

    def greet(m):
        pl.semaphore_signal(barrier, inc=1, device_id=(dp, m), device_id_type=MESH)

    every(
        lambda d, h, g: pl.semaphore_signal(
            barrier, inc=1, device_id=(d, z * n_x + h), device_id_type=MESH
        )
    )
    pl.when(has_below)(lambda: greet(mem - n_x))
    pl.when(has_above)(lambda: greet(mem + n_x))

    my_cols = pl.ds(pl.multiple_of(dp * cols, cols), cols)
    own = pltpu.make_async_copy(values_ref.at[:, my_cols], vals.at[z], own_sem)
    own.start()
    lists_got[me] = lists_ref[...]

    place_of = iota((spread, toks), 0)
    acc = jnp.zeros((spread, toks), jnp.float32)
    weights = w_ref[...].astype(jnp.float32)
    for k in range(topk):
        acc = jnp.where(pos_ref[k : k + 1, :] == place_of, weights[k : k + 1, :], acc)
    dense_w[...] = acc.astype(jnp.bfloat16)

    pl.semaphore_wait(barrier, group - 1 + has_below.astype(jnp.int32) + has_above.astype(jnp.int32))

    wide = cols // CHUNKS

    def line_copy(k, up, c):
        way = 1 if up else 0
        part = vals.at[k, :, pl.ds(c * wide, wide)]
        to = mem + n_x if up else mem - n_x
        return remote(part, part, line_ss.at[way, c, k], line_rs.at[c, k], dp, to)

    def pass_on(k, up, c):
        pl.when(has_above if up else has_below)(lambda: line_copy(k, up, c).start())

    def list_copy(d, h, g):
        return plane(lists_ref, lists_got.at[me], list_ss.at[0], list_rs.at[0], d, h)

    every(lambda d, h, g: list_copy(d, h, g).start())
    own.wait()
    for c in range(CHUNKS):
        pass_on(z, True, c)
        pass_on(z, False, c)

    def grad_copy(k, d, h, g):
        return plane(
            coded_mine.at[k, d, h], coded_got.at[k, me], grad_ss.at[k], grad_rs.at[k], d, h
        )

    def step_copy(k, d, h, g):
        return plane(step_mine.at[k, d], step_got.at[k, me], step_ss.at[k], step_rs.at[k], d, h)

    part = n_x * cap
    to_lane = iota((part, cap), 0) & (cap - 1) == iota((part, cap), 1)
    for i in range(n_z):
        k = jnp.where(z >= n_z // 2, i, n_z - 1 - i)
        weights_k = dense_w[pl.ds(pl.multiple_of(k * part, part), part), :]
        to_owner = iota((n_mem, part), 0) == (iota((n_mem, part), 1) >> bits) + k * n_x
        for d in range(n_dp):
            q, step = coded(
                jnp.dot(weights_k, cot_ref[:, d * cols : (d + 1) * cols], preferred_element_type=jnp.float32)
            )
            coded_mine[k, d] = q.reshape(n_x, cap, cols)
            step_mine[k, d] = jnp.dot(
                to_owner.astype(jnp.bfloat16),
                jnp.where(to_lane, step, 0.0).astype(jnp.bfloat16),
                preferred_element_type=jnp.float32,
            )
        every(lambda d, h, g: step_copy(k, d, h, g).start())
        every(lambda d, h, g: grad_copy(k, d, h, g).start())
    for k in range(n_z):
        step_got[k, me] = step_mine[k, dp]
        coded_got[k, me] = coded_mine[k, dp, x]

    others = pl.ds(0, group - 1)
    all_here(lists_got.at[others], list_rs.at[0])
    slots = group * cap
    fan = (iota((cap, slots), 1) & (cap - 1) == iota((cap, slots), 0)).astype(jnp.bfloat16)
    diag = iota((group, slots), 1) >> bits == iota((group, slots), 0)

    def along_lanes(table, m):
        pick = iota(table.shape, 1) == m
        part = jnp.sum(jnp.where(pick, table, 0.0), axis=1).astype(jnp.bfloat16)
        wide = jnp.dot(part, fan, preferred_element_type=jnp.float32)
        return jnp.sum(jnp.where(diag, wide, 0.0), axis=0, keepdims=True)

    row_of = iota((rows, slots), 0).astype(jnp.float32)

    def hot_of(k, c):
        lists_f = lists_got[...].astype(jnp.float32)
        hot[k] = (row_of == along_lanes(lists_f, k * n_x + x)).astype(jnp.bfloat16)
        return c

    lax.fori_loop(0, n_z, hot_of, 0)

    def val_copy(k, d, h, g):
        return plane(
            picked.at[k, g], arrived.at[k * n_x + x, :, my_cols], val_ss.at[k], val_rs.at[k], d, h
        )

    def select(k):
        got = lax.dot_general(
            hot[k], vals[k], (((0,), (0,)), ((), ())), preferred_element_type=jnp.float32
        )
        picked[k] = got.astype(jnp.bfloat16).reshape(group, cap, cols)
        every(lambda d, h, g: val_copy(k, d, h, g).start())
        arrived[k * n_x + x, :, my_cols] = picked[k, me]

    select(z)

    eye = iota((rows, rows), 0) == iota((rows, rows), 1)

    def gather_wait(k):
        all_here(step_got.at[k, others], step_rs.at[k])
        all_here(coded_got.at[k, others], grad_rs.at[k])

    def scaled_hot(k):
        return (hot[k].astype(jnp.float32) * along_lanes(step_got[k], k * n_x + x)).astype(jnp.bfloat16)

    def gathered(k, scaled, c):
        return decoded_sum(scaled, coded_got[k, :, :, c * wide : (c + 1) * wide].reshape(slots, wide))

    def sum_copies(k, up, c):
        to = mem + n_x if up else mem - n_x
        at = jnp.where(k == z + 1, n_z, k) if up else k
        return (
            remote(sum_step.at[c, k], sum_step_got.at[c, at], sum_ss.at[0, c, k], sum_rs.at[0, c, at], dp, to),
            remote(sum_coded.at[c, k], sum_got.at[c, at], sum_ss.at[1, c, k], sum_rs.at[1, c, at], dp, to),
        )

    def received(at, c):
        for src, dst, i in ((sum_step, sum_step_got, 0), (sum_coded, sum_got, 1)):
            remote(src.at[c, 0], dst.at[c, at], sum_ss.at[i, c, 0], sum_rs.at[i, c, at], dp, mem).wait_recv()
        scaled = jnp.where(eye, sum_step_got[c, at][0:1, :], 0.0).astype(jnp.bfloat16)
        return decoded_sum(scaled, sum_got[c, at])

    def relay(k, up, first):
        gather_wait(k)
        scaled = scaled_hot(k)
        for c in range(CHUNKS):
            sum_part[...] = gathered(k, scaled, c)

            @pl.when(jnp.logical_not(first))
            def _():
                sum_part[...] += received(k, c)

            q, step = coded(sum_part[...])
            sum_coded[c, k] = q
            sum_step[c, k] = jnp.broadcast_to(
                jnp.sum(jnp.where(eye, step, 0.0), axis=0, keepdims=True), sum_step.shape[2:]
            )
            for copy in sum_copies(k, up, c):
                copy.start()

    def take(k, up, c):
        line_copy(k, up, c).wait_recv()
        pass_on(k, up, c)

    def step_along(s, carry):
        @pl.when(s > 0)
        def _():
            from_below, from_above = z - s >= 0, z + s < n_z
            for c in range(CHUNKS):
                pl.when(from_below)(lambda: take(z - s, True, c))
                pl.when(from_above)(lambda: take(z + s, False, c))
            pl.when(from_below)(lambda: select(z - s))
            pl.when(from_above)(lambda: select(z + s))

        down = s - (n_z - 1 - z)
        pl.when((down >= 0) & (down < z))(lambda: relay(down, False, z == n_z - 1))
        up = n_z - 1 - s + z
        pl.when((up > z) & (up < n_z))(lambda: relay(up, True, z == 0))
        return carry

    lax.fori_loop(0, n_z, step_along, 0)
    gather_wait(z)
    own_hot = scaled_hot(z)
    for c in range(CHUNKS):
        sum_mine[:, c * wide : (c + 1) * wide] = gathered(z, own_hot, c)

    for k in range(n_z):
        all_here(picked.at[k, others], val_rs.at[k])

    def tokens(b, scores):
        at = pl.ds(pl.multiple_of(b * cols, cols), cols)
        table = arrived[:, :, at].reshape(spread, cols)
        out_ref[:, at] = lax.dot_general(
            dense_w[...], table, (((0,), (0,)), ((), ())), preferred_element_type=jnp.float32
        ).astype(out_ref.dtype)
        return scores + lax.dot_general(
            table, cot_ref[:, at], (((1,), (1,)), ((), ())), preferred_element_type=jnp.float32
        )

    scores = lax.fori_loop(0, n_dp, tokens, jnp.zeros((spread, toks), jnp.float32))
    for k in range(topk):
        wgrad_ref[k : k + 1, :] = jnp.sum(
            jnp.where(pos_ref[k : k + 1, :] == place_of, scores, 0.0), axis=0, keepdims=True
        )

    all_sent(lists_got.at[others], list_ss.at[0])

    def sent(k, carry):
        all_sent(step_got.at[k, others], step_ss.at[k])
        all_sent(coded_got.at[k, others], grad_ss.at[k])
        all_sent(picked.at[k, others], val_ss.at[k])
        for up in (False, True):
            @pl.when((has_above & (k <= z)) if up else (has_below & (k >= z)))
            def _():
                for c in range(CHUNKS):
                    line_copy(k, up, c).wait_send()
        return carry

    lax.fori_loop(0, n_z, sent, 0)

    for c in range(CHUNKS):
        at = slice(c * wide, (c + 1) * wide)

        @pl.when(has_above)
        def _():
            sum_mine[:, at] += received(z, c)

        @pl.when(has_below)
        def _():
            sum_mine[:, at] += received(n_z, c)

        vgrad_ref[:, at] = sum_mine[:, at]

    def sums_sent(k, carry):
        for up in (False, True):
            @pl.when((k > z) if up else (k < z))
            def _():
                for c in range(CHUNKS):
                    for copy in sum_copies(k, up, c):
                        copy.wait_send()
        return carry

    lax.fori_loop(0, n_z, sums_sent, 0)


def on_device(n_dp, n_mem, slot_weight, slot_pos, touched, values, cotangent):
    toks, topk = slot_pos.shape
    lists = touched[0]
    cap = lists.shape[1]
    rows, width = values.shape
    cols = width // n_dp
    n_x = 1
    while 4 * n_x * n_x <= n_mem:
        n_x *= 2
    n_z = n_mem // n_x
    group = n_dp * n_x
    f32, bf16, i16 = jnp.float32, jnp.bfloat16, jnp.int16
    dma = pltpu.SemaphoreType.DMA
    vmem = pl.BlockSpec(memory_space=pltpu.VMEM)
    out, wgrad, vgrad = pl.pallas_call(
        functools.partial(kernel, n_dp, n_mem, n_x),
        out_shape=(
            jax.ShapeDtypeStruct((toks, width), bf16),
            jax.ShapeDtypeStruct((topk, toks), f32),
            jax.ShapeDtypeStruct((rows, cols), f32),
        ),
        in_specs=[vmem, vmem, vmem, vmem, pl.BlockSpec(memory_space=pl.ANY)],
        out_specs=(vmem, vmem, vmem),
        scratch_shapes=[
            pltpu.VMEM((n_mem * cap, toks), bf16),
            pltpu.VMEM((n_z, n_dp, n_mem, cap), f32),
            pltpu.VMEM((n_z, group, n_mem, cap), f32),
            pltpu.VMEM((group, n_mem, cap), jnp.int32),
            pltpu.VMEM((n_z, n_dp, n_x, cap, cols), i16),
            pltpu.VMEM((n_z, group, cap, cols), i16),
            pltpu.VMEM((n_z, rows, group * cap), bf16),
            pltpu.VMEM((n_z, rows, cols), bf16),
            pltpu.VMEM((n_z, group, cap, cols), bf16),
            pltpu.VMEM((n_mem, cap, width), bf16),
            pltpu.VMEM((rows, cols), f32),
            pltpu.VMEM((rows, cols // CHUNKS), f32),
            pltpu.VMEM((CHUNKS, n_z, rows, cols // CHUNKS), i16),
            pltpu.VMEM((CHUNKS, n_z + 1, rows, cols // CHUNKS), i16),
            pltpu.VMEM((CHUNKS, n_z, 8, rows), f32),
            pltpu.VMEM((CHUNKS, n_z + 1, 8, rows), f32),
            dma((1,)), dma((1,)),
            dma((n_z,)), dma((n_z,)),
            dma((n_z,)), dma((n_z,)),
            dma((n_z,)), dma((n_z,)),
            dma((2, CHUNKS, n_z)), dma((CHUNKS, n_z)),
            dma((2, CHUNKS, n_z)), dma((2, CHUNKS, n_z + 1)),
            dma,
        ],
        compiler_params=pltpu.CompilerParams(
            collective_id=0, has_side_effects=True, vmem_limit_bytes=60 * 2**20
        ),
    )(lists, slot_pos.T, slot_weight.T, cotangent, values)
    return out, wgrad.T, vgrad


def solution(mesh):
    return jax.shard_map(
        functools.partial(on_device, mesh.shape["dp"], mesh.shape["mem"]),
        mesh=mesh,
        in_specs=(
            P(("dp", "mem"), None),
            P(("dp", "mem"), None),
            P(("dp", "mem"), None, None),
            P("mem", None),
            P(("dp", "mem"), None),
        ),
        out_specs=(P(("dp", "mem"), None), P(("dp", "mem"), None), P("mem", "dp")),
        check_vma=False,
    )
```

```python
import functools

import jax
import jax.numpy as jnp
from jax import lax
from jax.experimental import pallas as pl
from jax.experimental.pallas import tpu as pltpu
from jax.sharding import PartitionSpec as P

MESH = pl.DeviceIdType.MESH
STEPS = 32000.0
CHUNKS = 2


def iota(shape, axis):
    return lax.broadcasted_iota(jnp.int32, shape, axis)


def coded(x):
    top = jnp.max(jnp.abs(x), axis=1, keepdims=True)
    step = jnp.maximum(top * (1.0 / STEPS), 1e-30).astype(jnp.bfloat16).astype(jnp.float32)
    return jnp.round(x * (1.0 / step)).astype(jnp.int32).astype(jnp.int16), step


def pieces(q):
    full = q.astype(jnp.int32).astype(jnp.float32)
    high = full.astype(jnp.bfloat16)
    return high, (full - high.astype(jnp.float32)).astype(jnp.bfloat16)


def decoded_sum(hot, q):
    high, low = pieces(q)
    return jnp.dot(hot, high, preferred_element_type=jnp.float32) + jnp.dot(
        hot, low, preferred_element_type=jnp.float32
    )


def kernel(
    n_dp, n_mem, n_x,
    lists_ref, pos_ref, w_ref, cot_hbm, values_ref,
    out_hbm, wgrad_ref, vgrad_ref,
    cot_ref, out_ref, dense_wt, dense_w, step_mine, step_got, lists_got, coded_mine, coded_got, hot, vals, picked, arrived,
    sum_mine, sum_part, sum_coded, sum_got, sum_step, sum_step_got,
    list_ss, list_rs, step_ss, step_rs, grad_ss, grad_rs, val_ss, val_rs,
    line_ss, line_rs, sum_ss, sum_rs, own_sem,
):
    n_z = n_mem // n_x
    group = n_dp * n_x
    cap = lists_ref.shape[1]
    topk, toks = pos_ref.shape
    rows = values_ref.shape[0]
    cols = cot_hbm.shape[1] // n_dp
    spread = n_mem * cap
    bits = cap.bit_length() - 1
    dp = lax.axis_index("dp")
    mem = lax.axis_index("mem")
    z = mem // n_x
    x = lax.rem(mem, n_x)
    me = dp * n_x + x
    has_below, has_above = z > 0, z < n_z - 1

    def place(t):
        d = lax.rem(dp + 1 + t // n_x, n_dp)
        h = lax.rem(x + 1 + lax.rem(t, n_x), n_x)
        return d, h, d * n_x + h

    places = [place(t) for t in range(group - 1)] if group <= 8 else None

    def every(fn):
        if places is not None:
            for spot in places:
                fn(*spot)
            return

        def body(t, c):
            fn(*place(t))
            return c
        lax.fori_loop(0, group - 1, body, 0)

    def all_sent(like, sem):
        plane(like, like, sem, sem, dp, x).wait_send()

    def all_here(like, sem):
        plane(like, like, sem, sem, dp, x).wait_recv()

    def remote(src, dst, ss, rs, d, m):
        return pltpu.make_async_remote_copy(
            src_ref=src, dst_ref=dst, send_sem=ss, recv_sem=rs, device_id=(d, m), device_id_type=MESH
        )

    def plane(src, dst, ss, rs, d, h):
        return remote(src, dst, ss, rs, d, z * n_x + h)

    barrier = pltpu.get_barrier_semaphore()
    cot_in = pltpu.make_async_copy(cot_hbm, cot_ref, own_sem.at[1])
    cot_in.start()

    def greet(m):
        pl.semaphore_signal(barrier, inc=1, device_id=(dp, m), device_id_type=MESH)

    every(
        lambda d, h, g: pl.semaphore_signal(
            barrier, inc=1, device_id=(d, z * n_x + h), device_id_type=MESH
        )
    )
    pl.when(has_below)(lambda: greet(mem - n_x))
    pl.when(has_above)(lambda: greet(mem + n_x))

    my_cols = pl.ds(pl.multiple_of(dp * cols, cols), cols)
    own = pltpu.make_async_copy(values_ref.at[:, my_cols], vals.at[z], own_sem.at[0])
    own.start()
    lists_got[me] = lists_ref[...]

    place_of = iota((spread, toks), 0)
    acc = jnp.zeros((spread, toks), jnp.float32)
    weights = w_ref[...].astype(jnp.float32)
    for k in range(topk):
        acc = jnp.where(pos_ref[k : k + 1, :] == place_of, weights[k : k + 1, :], acc)
    dense_w[...] = acc.astype(jnp.bfloat16)

    pl.semaphore_wait(barrier, group - 1 + has_below.astype(jnp.int32) + has_above.astype(jnp.int32))

    wide = cols // CHUNKS

    def line_copy(k, up, c):
        way = 1 if up else 0
        part = vals.at[k, :, pl.ds(c * wide, wide)]
        to = mem + n_x if up else mem - n_x
        return remote(part, part, line_ss.at[way, c, k], line_rs.at[c, k], dp, to)

    def pass_on(k, up, c):
        pl.when(has_above if up else has_below)(lambda: line_copy(k, up, c).start())

    def list_copy(d, h, g):
        return plane(lists_ref, lists_got.at[me], list_ss.at[0], list_rs.at[0], d, h)

    every(lambda d, h, g: list_copy(d, h, g).start())
    own.wait()
    for c in range(CHUNKS):
        pass_on(z, True, c)
        pass_on(z, False, c)

    def grad_copy(k, d, h, g):
        return plane(
            coded_mine.at[k, d, h], coded_got.at[k, me], grad_ss.at[k], grad_rs.at[k], d, h
        )

    def step_copy(k, d, h, g):
        return plane(step_mine.at[k, d], step_got.at[k, me], step_ss.at[k], step_rs.at[k], d, h)

    cot_in.wait()
    part = n_x * cap
    to_lane = iota((part, cap), 0) & (cap - 1) == iota((part, cap), 1)
    for i in range(n_z):
        k = jnp.where(z >= n_z // 2, i, n_z - 1 - i)
        weights_k = dense_w[pl.ds(pl.multiple_of(k * part, part), part), :]
        to_owner = iota((n_mem, part), 0) == (iota((n_mem, part), 1) >> bits) + k * n_x
        for d in range(n_dp):
            q, step = coded(
                jnp.dot(weights_k, cot_ref[:, d * cols : (d + 1) * cols], preferred_element_type=jnp.float32)
            )
            coded_mine[k, d] = q.reshape(n_x, cap, cols)
            step_mine[k, d] = jnp.dot(
                to_owner.astype(jnp.bfloat16),
                jnp.where(to_lane, step, 0.0).astype(jnp.bfloat16),
                preferred_element_type=jnp.float32,
            )
        every(lambda d, h, g: step_copy(k, d, h, g).start())
        every(lambda d, h, g: grad_copy(k, d, h, g).start())
    for k in range(n_z):
        step_got[k, me] = step_mine[k, dp]
        coded_got[k, me] = coded_mine[k, dp, x]

    others = pl.ds(0, group - 1)
    all_here(lists_got.at[others], list_rs.at[0])
    slots = group * cap
    fan = (iota((cap, slots), 1) & (cap - 1) == iota((cap, slots), 0)).astype(jnp.bfloat16)
    diag = iota((group, slots), 1) >> bits == iota((group, slots), 0)

    def along_lanes(table, m):
        pick = iota(table.shape, 1) == m
        part = jnp.sum(jnp.where(pick, table, 0.0), axis=1).astype(jnp.bfloat16)
        wide = jnp.dot(part, fan, preferred_element_type=jnp.float32)
        return jnp.sum(jnp.where(diag, wide, 0.0), axis=0, keepdims=True)

    row_of = iota((rows, slots), 0).astype(jnp.float32)

    def hot_of(k, c):
        lists_f = lists_got[...].astype(jnp.float32)
        hot[k] = (row_of == along_lanes(lists_f, k * n_x + x)).astype(jnp.bfloat16)
        return c

    lax.fori_loop(0, n_z, hot_of, 0)

    def val_copy(k, d, h, g):
        return plane(
            picked.at[k, g], arrived.at[k * n_x + x, :, my_cols], val_ss.at[k], val_rs.at[k], d, h
        )

    def select(k):
        got = lax.dot_general(
            hot[k], vals[k], (((0,), (0,)), ((), ())), preferred_element_type=jnp.float32
        )
        picked[k] = got.astype(jnp.bfloat16).reshape(group, cap, cols)
        every(lambda d, h, g: val_copy(k, d, h, g).start())
        arrived[k * n_x + x, :, my_cols] = picked[k, me]

    select(z)

    dense_wt[...] = dense_w[...].astype(jnp.float32).T.astype(jnp.bfloat16)

    eye = iota((rows, rows), 0) == iota((rows, rows), 1)

    def gather_wait(k):
        all_here(step_got.at[k, others], step_rs.at[k])
        all_here(coded_got.at[k, others], grad_rs.at[k])

    def scaled_hot(k):
        return (hot[k].astype(jnp.float32) * along_lanes(step_got[k], k * n_x + x)).astype(jnp.bfloat16)

    def gathered(k, scaled, c):
        return decoded_sum(scaled, coded_got[k, :, :, c * wide : (c + 1) * wide].reshape(slots, wide))

    def sum_copies(k, up, c):
        to = mem + n_x if up else mem - n_x
        at = jnp.where(k == z + 1, n_z, k) if up else k
        return (
            remote(sum_step.at[c, k], sum_step_got.at[c, at], sum_ss.at[0, c, k], sum_rs.at[0, c, at], dp, to),
            remote(sum_coded.at[c, k], sum_got.at[c, at], sum_ss.at[1, c, k], sum_rs.at[1, c, at], dp, to),
        )

    def received(at, c):
        for src, dst, i in ((sum_step, sum_step_got, 0), (sum_coded, sum_got, 1)):
            remote(src.at[c, 0], dst.at[c, at], sum_ss.at[i, c, 0], sum_rs.at[i, c, at], dp, mem).wait_recv()
        scaled = jnp.where(eye, sum_step_got[c, at][0:1, :], 0.0).astype(jnp.bfloat16)
        return decoded_sum(scaled, sum_got[c, at])

    def relay(k, up, first):
        gather_wait(k)
        scaled = scaled_hot(k)
        for c in range(CHUNKS):
            sum_part[...] = gathered(k, scaled, c)

            @pl.when(jnp.logical_not(first))
            def _():
                sum_part[...] += received(k, c)

            q, step = coded(sum_part[...])
            sum_coded[c, k] = q
            sum_step[c, k] = jnp.broadcast_to(
                jnp.sum(jnp.where(eye, step, 0.0), axis=0, keepdims=True), sum_step.shape[2:]
            )
            for copy in sum_copies(k, up, c):
                copy.start()

    def take(k, up, c):
        line_copy(k, up, c).wait_recv()
        pass_on(k, up, c)

    def step_along(s, carry):
        @pl.when(s > 0)
        def _():
            from_below, from_above = z - s >= 0, z + s < n_z
            for c in range(CHUNKS):
                pl.when(from_below)(lambda: take(z - s, True, c))
                pl.when(from_above)(lambda: take(z + s, False, c))
            pl.when(from_below)(lambda: select(z - s))
            pl.when(from_above)(lambda: select(z + s))

        down = s - (n_z - 1 - z)
        pl.when((down >= 0) & (down < z))(lambda: relay(down, False, z == n_z - 1))
        up = n_z - 1 - s + z
        pl.when((up > z) & (up < n_z))(lambda: relay(up, True, z == 0))
        return carry

    lax.fori_loop(0, n_z, step_along, 0)
    gather_wait(z)
    own_hot = scaled_hot(z)
    for c in range(CHUNKS):
        sum_mine[:, c * wide : (c + 1) * wide] = gathered(z, own_hot, c)

    for k in range(n_z):
        all_here(picked.at[k, others], val_rs.at[k])

    def tokens(b, scores):
        at = pl.ds(pl.multiple_of(b * cols, cols), cols)
        table = arrived[:, :, at].reshape(spread, cols)
        out_ref[:, at] = jnp.dot(
            dense_wt[...], table, preferred_element_type=jnp.float32
        ).astype(out_ref.dtype)
        return scores + lax.dot_general(
            table, cot_ref[:, at], (((1,), (1,)), ((), ())), preferred_element_type=jnp.float32
        )

    scores = lax.fori_loop(0, n_dp, tokens, jnp.zeros((spread, toks), jnp.float32))
    out_back = pltpu.make_async_copy(out_ref, out_hbm, own_sem.at[1])
    out_back.start()
    for k in range(topk):
        wgrad_ref[k : k + 1, :] = jnp.sum(
            jnp.where(pos_ref[k : k + 1, :] == place_of, scores, 0.0), axis=0, keepdims=True
        )

    all_sent(lists_got.at[others], list_ss.at[0])

    def sent(k, carry):
        all_sent(step_got.at[k, others], step_ss.at[k])
        all_sent(coded_got.at[k, others], grad_ss.at[k])
        all_sent(picked.at[k, others], val_ss.at[k])
        for up in (False, True):
            @pl.when((has_above & (k <= z)) if up else (has_below & (k >= z)))
            def _():
                for c in range(CHUNKS):
                    line_copy(k, up, c).wait_send()
        return carry

    lax.fori_loop(0, n_z, sent, 0)

    for c in range(CHUNKS):
        at = slice(c * wide, (c + 1) * wide)

        @pl.when(has_above)
        def _():
            sum_mine[:, at] += received(z, c)

        @pl.when(has_below)
        def _():
            sum_mine[:, at] += received(n_z, c)

        vgrad_ref[:, at] = sum_mine[:, at]

    def sums_sent(k, carry):
        for up in (False, True):
            @pl.when((k > z) if up else (k < z))
            def _():
                for c in range(CHUNKS):
                    for copy in sum_copies(k, up, c):
                        copy.wait_send()
        return carry

    lax.fori_loop(0, n_z, sums_sent, 0)
    out_back.wait()


def on_device(n_dp, n_mem, slot_weight, slot_pos, touched, values, cotangent):
    toks, topk = slot_pos.shape
    lists = touched[0]
    cap = lists.shape[1]
    rows, width = values.shape
    cols = width // n_dp
    n_x = 1
    while 4 * n_x * n_x <= n_mem:
        n_x *= 2
    n_z = n_mem // n_x
    group = n_dp * n_x
    f32, bf16, i16 = jnp.float32, jnp.bfloat16, jnp.int16
    dma = pltpu.SemaphoreType.DMA
    vmem = pl.BlockSpec(memory_space=pltpu.VMEM)
    out, wgrad, vgrad = pl.pallas_call(
        functools.partial(kernel, n_dp, n_mem, n_x),
        out_shape=(
            jax.ShapeDtypeStruct((toks, width), bf16),
            jax.ShapeDtypeStruct((topk, toks), f32),
            jax.ShapeDtypeStruct((rows, cols), f32),
        ),
        in_specs=[vmem, vmem, vmem, pl.BlockSpec(memory_space=pl.ANY), pl.BlockSpec(memory_space=pl.ANY)],
        out_specs=(pl.BlockSpec(memory_space=pl.ANY), vmem, vmem),
        scratch_shapes=[
            pltpu.VMEM((toks, width), bf16),
            pltpu.VMEM((toks, width), bf16),
            pltpu.VMEM((toks, n_mem * cap), bf16),
            pltpu.VMEM((n_mem * cap, toks), bf16),
            pltpu.VMEM((n_z, n_dp, n_mem, cap), f32),
            pltpu.VMEM((n_z, group, n_mem, cap), f32),
            pltpu.VMEM((group, n_mem, cap), jnp.int32),
            pltpu.VMEM((n_z, n_dp, n_x, cap, cols), i16),
            pltpu.VMEM((n_z, group, cap, cols), i16),
            pltpu.VMEM((n_z, rows, group * cap), bf16),
            pltpu.VMEM((n_z, rows, cols), bf16),
            pltpu.VMEM((n_z, group, cap, cols), bf16),
            pltpu.VMEM((n_mem, cap, width), bf16),
            pltpu.VMEM((rows, cols), f32),
            pltpu.VMEM((rows, cols // CHUNKS), f32),
            pltpu.VMEM((CHUNKS, n_z, rows, cols // CHUNKS), i16),
            pltpu.VMEM((CHUNKS, n_z + 1, rows, cols // CHUNKS), i16),
            pltpu.VMEM((CHUNKS, n_z, 8, rows), f32),
            pltpu.VMEM((CHUNKS, n_z + 1, 8, rows), f32),
            dma((1,)), dma((1,)),
            dma((n_z,)), dma((n_z,)),
            dma((n_z,)), dma((n_z,)),
            dma((n_z,)), dma((n_z,)),
            dma((2, CHUNKS, n_z)), dma((CHUNKS, n_z)),
            dma((2, CHUNKS, n_z)), dma((2, CHUNKS, n_z + 1)),
            dma((2,)),
        ],
        compiler_params=pltpu.CompilerParams(
            collective_id=0, has_side_effects=True, vmem_limit_bytes=60 * 2**20
        ),
    )(lists, slot_pos.T, slot_weight.T, cotangent, values)
    return out, wgrad.T, vgrad


def solution(mesh):
    return jax.shard_map(
        functools.partial(on_device, mesh.shape["dp"], mesh.shape["mem"]),
        mesh=mesh,
        in_specs=(
            P(("dp", "mem"), None),
            P(("dp", "mem"), None),
            P(("dp", "mem"), None, None),
            P("mem", None),
            P(("dp", "mem"), None),
        ),
        out_specs=(P(("dp", "mem"), None), P(("dp", "mem"), None), P("mem", "dp")),
        check_vma=False,
    )
```

```python
import functools

import jax
import jax.numpy as jnp
from jax import lax
from jax.experimental import pallas as pl
from jax.experimental.pallas import tpu as pltpu
from jax.sharding import PartitionSpec as P

MESH = pl.DeviceIdType.MESH
STEPS = 32000.0
CHUNKS = 4


def iota(shape, axis):
    return lax.broadcasted_iota(jnp.int32, shape, axis)


def coded(x):
    top = jnp.max(jnp.abs(x), axis=1, keepdims=True)
    step = jnp.maximum(top * (1.0 / STEPS), 1e-30).astype(jnp.bfloat16).astype(jnp.float32)
    return jnp.round(x * (1.0 / step)).astype(jnp.int32).astype(jnp.int16), step


def pieces(q):
    full = q.astype(jnp.int32).astype(jnp.float32)
    high = full.astype(jnp.bfloat16)
    return high, (full - high.astype(jnp.float32)).astype(jnp.bfloat16)


def decoded_sum(hot, q):
    high, low = pieces(q)
    return jnp.dot(hot, high, preferred_element_type=jnp.float32) + jnp.dot(
        hot, low, preferred_element_type=jnp.float32
    )


def kernel(
    n_dp, n_mem, n_x,
    lists_ref, pos_ref, w_ref, cot_hbm, values_ref,
    out_hbm, wgrad_ref, vgrad_ref,
    cot_ref, out_ref, dense_wt, dense_w, step_mine, step_got, lists_got, coded_mine, coded_got, hot, vals, picked, arrived,
    sum_mine, sum_part, sum_coded, sum_got, sum_step, sum_step_got,
    list_ss, list_rs, step_ss, step_rs, grad_ss, grad_rs, val_ss, val_rs,
    line_ss, line_rs, sum_ss, sum_rs, own_sem,
):
    n_z = n_mem // n_x
    group = n_dp * n_x
    cap = lists_ref.shape[1]
    topk, toks = pos_ref.shape
    rows = values_ref.shape[0]
    cols = cot_hbm.shape[1] // n_dp
    spread = n_mem * cap
    bits = cap.bit_length() - 1
    dp = lax.axis_index("dp")
    mem = lax.axis_index("mem")
    z = mem // n_x
    x = lax.rem(mem, n_x)
    me = dp * n_x + x
    has_below, has_above = z > 0, z < n_z - 1

    def place(t):
        d = lax.rem(dp + 1 + t // n_x, n_dp)
        h = lax.rem(x + 1 + lax.rem(t, n_x), n_x)
        return d, h, d * n_x + h

    places = [place(t) for t in range(group - 1)] if group <= 8 else None

    def every(fn):
        if places is not None:
            for spot in places:
                fn(*spot)
            return

        def body(t, c):
            fn(*place(t))
            return c
        lax.fori_loop(0, group - 1, body, 0)

    def all_sent(like, sem):
        plane(like, like, sem, sem, dp, x).wait_send()

    def all_here(like, sem):
        plane(like, like, sem, sem, dp, x).wait_recv()

    def remote(src, dst, ss, rs, d, m):
        return pltpu.make_async_remote_copy(
            src_ref=src, dst_ref=dst, send_sem=ss, recv_sem=rs, device_id=(d, m), device_id_type=MESH
        )

    def plane(src, dst, ss, rs, d, h):
        return remote(src, dst, ss, rs, d, z * n_x + h)

    barrier = pltpu.get_barrier_semaphore()
    cot_in = pltpu.make_async_copy(cot_hbm, cot_ref, own_sem.at[1])
    cot_in.start()

    def greet(m):
        pl.semaphore_signal(barrier, inc=1, device_id=(dp, m), device_id_type=MESH)

    every(
        lambda d, h, g: pl.semaphore_signal(
            barrier, inc=1, device_id=(d, z * n_x + h), device_id_type=MESH
        )
    )
    pl.when(has_below)(lambda: greet(mem - n_x))
    pl.when(has_above)(lambda: greet(mem + n_x))

    my_cols = pl.ds(pl.multiple_of(dp * cols, cols), cols)
    own = pltpu.make_async_copy(values_ref.at[:, my_cols], vals.at[z], own_sem.at[0])
    own.start()
    lists_got[me] = lists_ref[...]

    place_of = iota((spread, toks), 0)
    acc = jnp.zeros((spread, toks), jnp.float32)
    weights = w_ref[...].astype(jnp.float32)
    for k in range(topk):
        acc = jnp.where(pos_ref[k : k + 1, :] == place_of, weights[k : k + 1, :], acc)
    dense_w[...] = acc.astype(jnp.bfloat16)

    pl.semaphore_wait(barrier, group - 1 + has_below.astype(jnp.int32) + has_above.astype(jnp.int32))

    wide = cols // CHUNKS

    def line_copy(k, up, c):
        way = 1 if up else 0
        part = vals.at[k, :, pl.ds(c * wide, wide)]
        to = mem + n_x if up else mem - n_x
        return remote(part, part, line_ss.at[way, c, k], line_rs.at[c, k], dp, to)

    def pass_on(k, up, c):
        pl.when(has_above if up else has_below)(lambda: line_copy(k, up, c).start())

    def list_copy(d, h, g):
        return plane(lists_ref, lists_got.at[me], list_ss.at[0], list_rs.at[0], d, h)

    every(lambda d, h, g: list_copy(d, h, g).start())
    own.wait()
    for c in range(CHUNKS):
        pass_on(z, True, c)
        pass_on(z, False, c)

    def grad_copy(k, d, h, g):
        return plane(
            coded_mine.at[k, d, h], coded_got.at[k, me], grad_ss.at[k], grad_rs.at[k], d, h
        )

    def step_copy(k, d, h, g):
        return plane(step_mine.at[k, d], step_got.at[k, me], step_ss.at[k], step_rs.at[k], d, h)

    cot_in.wait()
    part = n_x * cap
    to_lane = iota((part, cap), 0) & (cap - 1) == iota((part, cap), 1)
    for i in range(n_z):
        k = jnp.where(z >= n_z // 2, i, n_z - 1 - i)
        weights_k = dense_w[pl.ds(pl.multiple_of(k * part, part), part), :]
        to_owner = iota((n_mem, part), 0) == (iota((n_mem, part), 1) >> bits) + k * n_x
        for d in range(n_dp):
            q, step = coded(
                jnp.dot(weights_k, cot_ref[:, d * cols : (d + 1) * cols], preferred_element_type=jnp.float32)
            )
            coded_mine[k, d] = q.reshape(n_x, cap, cols)
            step_mine[k, d] = jnp.dot(
                to_owner.astype(jnp.bfloat16),
                jnp.where(to_lane, step, 0.0).astype(jnp.bfloat16),
                preferred_element_type=jnp.float32,
            )
        every(lambda d, h, g: step_copy(k, d, h, g).start())
        every(lambda d, h, g: grad_copy(k, d, h, g).start())
    for k in range(n_z):
        step_got[k, me] = step_mine[k, dp]
        coded_got[k, me] = coded_mine[k, dp, x]

    others = pl.ds(0, group - 1)
    all_here(lists_got.at[others], list_rs.at[0])
    slots = group * cap
    fan = (iota((cap, slots), 1) & (cap - 1) == iota((cap, slots), 0)).astype(jnp.bfloat16)
    diag = iota((group, slots), 1) >> bits == iota((group, slots), 0)

    def along_lanes(table, m):
        pick = iota(table.shape, 1) == m
        part = jnp.sum(jnp.where(pick, table, 0.0), axis=1).astype(jnp.bfloat16)
        wide = jnp.dot(part, fan, preferred_element_type=jnp.float32)
        return jnp.sum(jnp.where(diag, wide, 0.0), axis=0, keepdims=True)

    row_of = iota((rows, slots), 0).astype(jnp.float32)

    def hot_of(k, c):
        lists_f = lists_got[...].astype(jnp.float32)
        hot[k] = (row_of == along_lanes(lists_f, k * n_x + x)).astype(jnp.bfloat16)
        return c

    lax.fori_loop(0, n_z, hot_of, 0)

    def val_copy(k, d, h, g):
        return plane(
            picked.at[k, g], arrived.at[k * n_x + x, :, my_cols], val_ss.at[k], val_rs.at[k], d, h
        )

    def select(k):
        got = lax.dot_general(
            hot[k], vals[k], (((0,), (0,)), ((), ())), preferred_element_type=jnp.float32
        )
        picked[k] = got.astype(jnp.bfloat16).reshape(group, cap, cols)
        every(lambda d, h, g: val_copy(k, d, h, g).start())
        arrived[k * n_x + x, :, my_cols] = picked[k, me]

    select(z)

    dense_wt[...] = dense_w[...].astype(jnp.float32).T.astype(jnp.bfloat16)

    eye = iota((rows, rows), 0) == iota((rows, rows), 1)

    def gather_wait(k):
        all_here(step_got.at[k, others], step_rs.at[k])
        all_here(coded_got.at[k, others], grad_rs.at[k])

    def scaled_hot(k):
        return (hot[k].astype(jnp.float32) * along_lanes(step_got[k], k * n_x + x)).astype(jnp.bfloat16)

    def gathered(k, scaled, c):
        return decoded_sum(scaled, coded_got[k, :, :, c * wide : (c + 1) * wide].reshape(slots, wide))

    def sum_copies(k, up, c):
        to = mem + n_x if up else mem - n_x
        at = jnp.where(k == z + 1, n_z, k) if up else k
        return (
            remote(sum_step.at[c, k], sum_step_got.at[c, at], sum_ss.at[0, c, k], sum_rs.at[0, c, at], dp, to),
            remote(sum_coded.at[c, k], sum_got.at[c, at], sum_ss.at[1, c, k], sum_rs.at[1, c, at], dp, to),
        )

    def received(at, c):
        for src, dst, i in ((sum_step, sum_step_got, 0), (sum_coded, sum_got, 1)):
            remote(src.at[c, 0], dst.at[c, at], sum_ss.at[i, c, 0], sum_rs.at[i, c, at], dp, mem).wait_recv()
        scaled = jnp.where(eye, sum_step_got[c, at][0:1, :], 0.0).astype(jnp.bfloat16)
        return decoded_sum(scaled, sum_got[c, at])

    def relay(k, up, first):
        gather_wait(k)
        scaled = scaled_hot(k)
        for c in range(CHUNKS):
            sum_part[...] = gathered(k, scaled, c)

            @pl.when(jnp.logical_not(first))
            def _():
                sum_part[...] += received(k, c)

            q, step = coded(sum_part[...])
            sum_coded[c, k] = q
            sum_step[c, k] = jnp.broadcast_to(
                jnp.sum(jnp.where(eye, step, 0.0), axis=0, keepdims=True), sum_step.shape[2:]
            )
            for copy in sum_copies(k, up, c):
                copy.start()

    def take(k, up, c):
        line_copy(k, up, c).wait_recv()
        pass_on(k, up, c)

    def step_along(s, carry):
        @pl.when(s > 0)
        def _():
            from_below, from_above = z - s >= 0, z + s < n_z
            for c in range(CHUNKS):
                pl.when(from_below)(lambda: take(z - s, True, c))
                pl.when(from_above)(lambda: take(z + s, False, c))
            pl.when(from_below)(lambda: select(z - s))
            pl.when(from_above)(lambda: select(z + s))

        down = s - (n_z - 1 - z)
        pl.when((down >= 0) & (down < z))(lambda: relay(down, False, z == n_z - 1))
        up = n_z - 1 - s + z
        pl.when((up > z) & (up < n_z))(lambda: relay(up, True, z == 0))
        return carry

    lax.fori_loop(0, n_z, step_along, 0)
    gather_wait(z)
    own_hot = scaled_hot(z)
    for c in range(CHUNKS):
        sum_mine[:, c * wide : (c + 1) * wide] = gathered(z, own_hot, c)

    for k in range(n_z):
        all_here(picked.at[k, others], val_rs.at[k])

    def tokens(b, scores):
        at = pl.ds(pl.multiple_of(b * cols, cols), cols)
        table = arrived[:, :, at].reshape(spread, cols)
        out_ref[:, at] = jnp.dot(
            dense_wt[...], table, preferred_element_type=jnp.float32
        ).astype(out_ref.dtype)
        return scores + lax.dot_general(
            table, cot_ref[:, at], (((1,), (1,)), ((), ())), preferred_element_type=jnp.float32
        )

    scores = lax.fori_loop(0, n_dp, tokens, jnp.zeros((spread, toks), jnp.float32))
    out_back = pltpu.make_async_copy(out_ref, out_hbm, own_sem.at[1])
    out_back.start()
    for k in range(topk):
        wgrad_ref[k : k + 1, :] = jnp.sum(
            jnp.where(pos_ref[k : k + 1, :] == place_of, scores, 0.0), axis=0, keepdims=True
        )

    all_sent(lists_got.at[others], list_ss.at[0])

    def sent(k, carry):
        all_sent(step_got.at[k, others], step_ss.at[k])
        all_sent(coded_got.at[k, others], grad_ss.at[k])
        all_sent(picked.at[k, others], val_ss.at[k])
        for up in (False, True):
            @pl.when((has_above & (k <= z)) if up else (has_below & (k >= z)))
            def _():
                for c in range(CHUNKS):
                    line_copy(k, up, c).wait_send()
        return carry

    lax.fori_loop(0, n_z, sent, 0)

    for c in range(CHUNKS):
        at = slice(c * wide, (c + 1) * wide)

        @pl.when(has_above)
        def _():
            sum_mine[:, at] += received(z, c)

        @pl.when(has_below)
        def _():
            sum_mine[:, at] += received(n_z, c)

        vgrad_ref[:, at] = sum_mine[:, at]

    def sums_sent(k, carry):
        for up in (False, True):
            @pl.when((k > z) if up else (k < z))
            def _():
                for c in range(CHUNKS):
                    for copy in sum_copies(k, up, c):
                        copy.wait_send()
        return carry

    lax.fori_loop(0, n_z, sums_sent, 0)
    out_back.wait()


def on_device(n_dp, n_mem, slot_weight, slot_pos, touched, values, cotangent):
    toks, topk = slot_pos.shape
    lists = touched[0]
    cap = lists.shape[1]
    rows, width = values.shape
    cols = width // n_dp
    n_x = 1
    while 4 * n_x * n_x <= n_mem:
        n_x *= 2
    n_z = n_mem // n_x
    group = n_dp * n_x
    f32, bf16, i16 = jnp.float32, jnp.bfloat16, jnp.int16
    dma = pltpu.SemaphoreType.DMA
    vmem = pl.BlockSpec(memory_space=pltpu.VMEM)
    out, wgrad, vgrad = pl.pallas_call(
        functools.partial(kernel, n_dp, n_mem, n_x),
        out_shape=(
            jax.ShapeDtypeStruct((toks, width), bf16),
            jax.ShapeDtypeStruct((topk, toks), f32),
            jax.ShapeDtypeStruct((rows, cols), f32),
        ),
        in_specs=[vmem, vmem, vmem, pl.BlockSpec(memory_space=pl.ANY), pl.BlockSpec(memory_space=pl.ANY)],
        out_specs=(pl.BlockSpec(memory_space=pl.ANY), vmem, vmem),
        scratch_shapes=[
            pltpu.VMEM((toks, width), bf16),
            pltpu.VMEM((toks, width), bf16),
            pltpu.VMEM((toks, n_mem * cap), bf16),
            pltpu.VMEM((n_mem * cap, toks), bf16),
            pltpu.VMEM((n_z, n_dp, n_mem, cap), f32),
            pltpu.VMEM((n_z, group, n_mem, cap), f32),
            pltpu.VMEM((group, n_mem, cap), jnp.int32),
            pltpu.VMEM((n_z, n_dp, n_x, cap, cols), i16),
            pltpu.VMEM((n_z, group, cap, cols), i16),
            pltpu.VMEM((n_z, rows, group * cap), bf16),
            pltpu.VMEM((n_z, rows, cols), bf16),
            pltpu.VMEM((n_z, group, cap, cols), bf16),
            pltpu.VMEM((n_mem, cap, width), bf16),
            pltpu.VMEM((rows, cols), f32),
            pltpu.VMEM((rows, cols // CHUNKS), f32),
            pltpu.VMEM((CHUNKS, n_z, rows, cols // CHUNKS), i16),
            pltpu.VMEM((CHUNKS, n_z + 1, rows, cols // CHUNKS), i16),
            pltpu.VMEM((CHUNKS, n_z, 8, rows), f32),
            pltpu.VMEM((CHUNKS, n_z + 1, 8, rows), f32),
            dma((1,)), dma((1,)),
            dma((n_z,)), dma((n_z,)),
            dma((n_z,)), dma((n_z,)),
            dma((n_z,)), dma((n_z,)),
            dma((2, CHUNKS, n_z)), dma((CHUNKS, n_z)),
            dma((2, CHUNKS, n_z)), dma((2, CHUNKS, n_z + 1)),
            dma((2,)),
        ],
        compiler_params=pltpu.CompilerParams(
            collective_id=0, has_side_effects=True, vmem_limit_bytes=60 * 2**20
        ),
    )(lists, slot_pos.T, slot_weight.T, cotangent, values)
    return out, wgrad.T, vgrad


def solution(mesh):
    return jax.shard_map(
        functools.partial(on_device, mesh.shape["dp"], mesh.shape["mem"]),
        mesh=mesh,
        in_specs=(
            P(("dp", "mem"), None),
            P(("dp", "mem"), None),
            P(("dp", "mem"), None, None),
            P("mem", None),
            P(("dp", "mem"), None),
        ),
        out_specs=(P(("dp", "mem"), None), P(("dp", "mem"), None), P("mem", "dp")),
        check_vma=False,
    )
```
